32 devices in a mesh: groups: 2 (over x), seq: 16 (over z, y, core).
Axes of the slice: x: 2, y: 2, z: 4, core: 2. Of those that a mesh axis runs over, the one named last changes fastest.
Arguments:
- queries: bfloat16 [8192, 2048], P(('groups', 'seq')), parts along dimension 0, may hold values from -14 to 14
- ctx_keys: bfloat16 [8192, 512], P(('groups', 'seq')), parts along dimension 0, may hold values from -11.5 to 11.5
- ctx_values: bfloat16 [8192, 512], P(('groups', 'seq')), parts along dimension 0, may hold values from -5 to 5
- store_keys: bfloat16 [512, 128, 512], P(('groups', 'seq')), parts along dimension 0, may hold values from -11.5 to 11.5
- store_values: bfloat16 [512, 128, 512], P(('groups', 'seq')), parts along dimension 0, may hold values from -5 to 5
- block_ids: int32 [32, 32], P(('groups', 'seq')), parts along dimension 0, may hold values from 0 to 255, as said below
- block_slot: int32 [512], P('groups'), parts along dimension 0, may hold values from 0 to 255, as said below
- gate_logit: float32 [16], replicated, may hold values from -2 to 2
Outputs:
- mixed: bfloat16 [8192, 2048], P(('groups', 'seq')), parts along dimension 0
The draws below stay inside these ranges and needn't reach their ends.
There are 2 independent parts, one for each index of `groups`. The reference program is written for one: setup_inputs(seed, part) draws one part's arguments, and reference() takes and returns one part's arrays. A program takes and returns all parts, laid end to end along the dimension named above; an argument that names none is the same for every part. Nothing has to cross between parts.
Inputs may be any that keep to these rules, and one draw needn't show every extreme that they name: block_slot is a permutation of 0 to 255; memory block b lies on seq index block_slot[b] // 16 at local position block_slot[b] % 16. `block_ids`: the 32 ids of one row are distinct; at most 2 of them lie on any one seq index, and in every draw some seq index holds exactly 2 blocks of every row.
All inputs are finite; a program needn't handle non-finite values.
Results may differ from the reference program's by a relative error of at most 0.0052.
Values may be sent and summed in bfloat16 or wider, within the bound.
No kernel may reach another device: no remote copies, remote signals or barrier semaphores. Data moves between devices by JAX's collectives and lax.ppermute only.
A program may use at most 192 MiB of HBM per device.

```python
import jax
import jax.numpy as jnp
from jax import lax

H = 16
KVH = 4
HD = 128
QBLK = 256
MROWS = 128
TOPM = 32
CAP = 2
MEM_DEV = 16
TOKENS = 4096
NQB = 16
MEM_BLOCKS = 256


def route_tables(key):
    base = jax.random.fold_in(key, 4242)
    key_perm = jax.random.fold_in(base, 1)
    key_hot = jax.random.fold_in(base, 2)
    key_popular = jax.random.fold_in(base, 3)
    key_score = jax.random.fold_in(base, 4)
    key_first = jax.random.fold_in(base, 5)
    key_stride = jax.random.fold_in(base, 6)
    owners_count = MEM_BLOCKS // MEM_DEV
    slot_of = jax.random.permutation(key_perm, MEM_BLOCKS).astype(jnp.int32)
    id_of_slot = jnp.argsort(slot_of).astype(jnp.int32)
    hottest = jax.random.randint(key_hot, (), 0, owners_count)
    popular = jax.random.randint(key_popular, (owners_count,), 0, 2 ** 19)
    candidates = jnp.arange(owners_count * CAP, dtype=jnp.int32)
    cand_owner = candidates // CAP
    score = jax.random.randint(key_score, (NQB, owners_count * CAP), 0, 2 ** 19) + popular[cand_owner][None, :]
    score = score + jnp.where(cand_owner == hottest, 2 ** 21, 0)[None, :]
    score = score * (owners_count * CAP) + candidates[None, :]
    ignored, chosen = lax.top_k(score, TOPM)
    owner = chosen // CAP
    copy_no = chosen % CAP
    first = jax.random.randint(key_first, (NQB, owners_count), 0, MEM_DEV)
    stride = jax.random.randint(key_stride, (NQB, owners_count), 1, MEM_DEV)
    local = (jnp.take_along_axis(first, owner, axis=1) + copy_no * jnp.take_along_axis(stride, owner, axis=1)) % MEM_DEV
    slots = owner * MEM_DEV + local
    return (slot_of, id_of_slot[slots].astype(jnp.int32))


def draw_block_ids(key, part):
    return route_tables(key)[1]


def draw_block_slot(key, part):
    return route_tables(key)[0]


def draw_queries(key, part):
    inner = jax.random.fold_in(key, 11)
    field = jnp.clip(2.5 * jax.random.normal(inner, (TOKENS, H * HD), jnp.float32), -14.0, 14.0)
    return field.astype(jnp.bfloat16)


def draw_ctx_keys(key, part):
    inner = jax.random.fold_in(key, 12)
    field = jnp.clip(jax.random.normal(inner, (TOKENS, KVH * HD), jnp.float32), -4.0, 4.0)
    return field.astype(jnp.bfloat16)


def draw_store_keys(key, part):
    inner = jax.random.fold_in(key, 13)
    field = jnp.clip(jax.random.normal(inner, (MEM_BLOCKS, MROWS, KVH * HD), jnp.float32), -4.0, 4.0)
    return field.astype(jnp.bfloat16)


def block_scale(stream_key, shape, pieces, smallest, high):
    loudness, own = 1.0, jax.random.fold_in(stream_key, 6)
    for position, shards_of in pieces:
        draws = jnp.exp(jax.random.uniform(jax.random.fold_in(own, position), (shards_of,), jnp.float32, smallest / len(pieces), high / len(pieces)))
        loudness = loudness * jnp.repeat(draws, shape[position] // shards_of).reshape([-1 if axis == position else 1 for axis in range(len(shape))])
    return loudness


def normal_values(stream_key, shape, scale, limit, pieces=(), held_as=jnp.bfloat16):
    factor_of = block_scale(stream_key, shape, pieces, -0.22, 0.18) if pieces else 1.0
    array = jax.random.normal(stream_key, shape, jnp.float32) * scale * factor_of
    return jnp.minimum(jnp.maximum(array, -limit), limit).astype(held_as)


def setup_inputs(seed: int = 0, part: int = 0) -> dict:
    splits = jax.random.split(jax.random.key(seed), 9)
    part_keys = jax.random.split(jax.random.fold_in(splits[8], part), 9)
    queries = draw_queries(jax.random.fold_in(jax.random.fold_in(splits[8], part), 71), part)
    ctx_keys = draw_ctx_keys(jax.random.fold_in(jax.random.fold_in(splits[8], part), 71), part)
    ctx_values = normal_values(part_keys[2], (TOKENS, KVH * HD), 1.0, 5.0, ((0, 16),))
    store_keys = draw_store_keys(jax.random.fold_in(jax.random.fold_in(splits[8], part), 71), part)
    store_values = normal_values(part_keys[4], (MEM_BLOCKS, MROWS, KVH * HD), 1.0, 5.0, ((0, 16),))
    block_ids = draw_block_ids(jax.random.fold_in(jax.random.fold_in(splits[8], part), 71), part)
    block_slot = draw_block_slot(jax.random.fold_in(jax.random.fold_in(splits[8], part), 71), part)
    gate_logit = jnp.clip(jax.random.uniform(splits[7], (H,), jnp.float32, -2.0, 2.0), -2.0, 2.0)
    return {"queries": queries, "ctx_keys": ctx_keys, "ctx_values": ctx_values, "store_keys": store_keys, "store_values": store_values, "block_ids": block_ids, "block_slot": block_slot, "gate_logit": gate_logit}


def attend(query_rows, key_rows, value_rows, allowed):
    row_count = query_rows.shape[0]
    query_heads = query_rows.astype(jnp.float32).reshape(row_count, KVH, H // KVH, HD)
    key_heads = key_rows.astype(jnp.float32).reshape(-1, KVH, HD)
    value_heads = value_rows.astype(jnp.float32).reshape(-1, KVH, HD)
    scores = jnp.einsum("rhgd,khd->hgrk", query_heads, key_heads) * (HD ** -0.5)
    if allowed is not None:
        scores = jnp.where(allowed[None, None], scores, -1e30)
    row_max = jnp.max(scores, axis=-1, keepdims=True)
    probs = jnp.exp(scores - row_max)
    total = jnp.sum(probs, axis=-1)
    rounded = lax.optimization_barrier(probs.astype(jnp.bfloat16)).astype(jnp.float32)
    weighted = jnp.einsum("hgrk,khd->hgrd", rounded, value_heads)
    result = weighted / total[..., None]
    return jnp.transpose(result, (2, 0, 1, 3)).reshape(row_count, H * HD).astype(jnp.bfloat16)


def reference(queries, ctx_keys, ctx_values, store_keys, store_values, block_ids, block_slot, gate_logit):
    positions = jnp.arange(TOKENS, dtype=jnp.int32)
    gate = jnp.repeat(jax.nn.sigmoid(gate_logit.astype(jnp.float32)), HD)

    def one_block(block_no):
        start = (block_no * QBLK).astype(jnp.int32)
        query_rows = lax.dynamic_slice_in_dim(queries, start, QBLK, 0)
        query_pos = start + jnp.arange(QBLK, dtype=jnp.int32)
        allowed = positions[None, :] <= query_pos[:, None]
        context = attend(query_rows, ctx_keys, ctx_values, allowed)
        slots = block_slot[block_ids[block_no]]
        memory_keys = store_keys[slots].reshape(TOPM * MROWS, KVH * HD)
        memory_values = store_values[slots].reshape(TOPM * MROWS, KVH * HD)
        memory = attend(query_rows, memory_keys, memory_values, None)
        memory_wide = lax.optimization_barrier(memory).astype(jnp.float32)
        context_wide = lax.optimization_barrier(context).astype(jnp.float32)
        return (gate * memory_wide + (1.0 - gate) * context_wide).astype(jnp.bfloat16)

    blocks = lax.map(one_block, jnp.arange(NQB, dtype=jnp.int32))
    return blocks.reshape(TOKENS, H * HD)
```

```python
import functools

import jax
import jax.numpy as jnp
from jax import lax
from jax.experimental import pallas as pl
from jax.experimental.pallas import tpu as pltpu
from jax.sharding import PartitionSpec as P

H = 16
KVH = 4
HD = 128
QBLK = 256
MROWS = 128
TOPM = 32
CAP = 2
G = H // KVH
WITHIN = 4
LOG2E = 1.4426950408889634
SCALE = HD**-0.5 * LOG2E
MASKED = -1e30
QW = G * HD
STAGES = ((0, 1), (1, 1), (2, 1), (3, 1))


def request_table(slots, owners_count, local_count):
    entries = slots.shape[0]
    owner = slots // local_count
    local = slots % local_count
    order = jnp.arange(entries, dtype=jnp.int32)
    earlier = (owner[:, None] == owner[None, :]) & (order[None, :] < order[:, None])
    rank = jnp.sum(earlier.astype(jnp.int32), axis=1)
    chosen = (owner[:, None, None] == jnp.arange(owners_count, dtype=jnp.int32)[None, :, None]) & (
        rank[:, None, None] == jnp.arange(CAP, dtype=jnp.int32)[None, None, :]
    )
    return jnp.sum(jnp.where(chosen, local[:, None, None] + 1, 0), axis=0) - 1


def lookup_slots(wanted_ids, block_slot):
    hits = wanted_ids[..., None] == jnp.arange(block_slot.shape[0], dtype=jnp.int32)
    return jnp.sum(jnp.where(hits, block_slot, 0), axis=-1)


def attend_heads(q, k, v, allowed, out_ref, lse_rows):
    keys = k.shape[0]
    vx = jnp.concatenate([v, jnp.ones((keys, HD), jnp.bfloat16)], axis=1)
    lane = lax.broadcasted_iota(jnp.int32, (QBLK, HD), 1)
    for g in range(G):
        s = lax.dot_general(
            q[:, g * HD : (g + 1) * HD], k, (((1,), (1,)), ((), ())), preferred_element_type=jnp.float32
        )
        s = s * SCALE
        if allowed is not None:
            s = jnp.where(allowed, s, MASKED)
        m = jnp.max(s, axis=1, keepdims=True)
        p = jnp.exp2(s - m).astype(jnp.bfloat16)
        o = jnp.dot(p, vx, preferred_element_type=jnp.float32)
        total = o[:, HD:]
        out_ref[0, :, g * HD : (g + 1) * HD] = (o[:, :HD] / total).astype(jnp.bfloat16)
        lse_rows = jnp.where(lane == g, m + jnp.log2(total), lse_rows)
    return lse_rows


def ctx_kernel(info, q_ref, k0, k1, k2, k3, v0, v1, v2, v3, out_ref, lse_ref):
    slot = pl.program_id(1)
    plane, within = info[0], info[1]
    target = info[2 + slot]

    def run(allowed):
        k = jnp.concatenate([k0[...], k1[...], k2[...], k3[...]], axis=0)
        v = jnp.concatenate([v0[...], v1[...], v2[...], v3[...]], axis=0)
        rows = attend_heads(q_ref[0], k, v, allowed, out_ref, jnp.zeros((QBLK, HD), jnp.float32))
        lse_ref[0, 0] = rows.T[:8]

    @pl.when(target > plane)
    def _():
        run(None)

    @pl.when(target == plane)
    def _():
        keys = WITHIN * QBLK
        col = lax.broadcasted_iota(jnp.int32, (QBLK, keys), 1)
        row = lax.broadcasted_iota(jnp.int32, (QBLK, keys), 0)
        key_pos = jnp.bitwise_xor(col // QBLK, within) * QBLK + col % QBLK
        run(key_pos <= within * QBLK + row)

    @pl.when(target < plane)
    def _():
        out_ref[...] = jnp.zeros_like(out_ref)
        lse_ref[...] = jnp.full_like(lse_ref, MASKED)


def mem_kernel(masked, info, q_ref, k0, k1, k2, k3, v0, v1, v2, v3, ctx_lse_ref, out_ref, lse_ref, kbuf, vbuf):
    slot = pl.program_id(1)
    allowed = None
    keys = WITHIN * CAP * MROWS
    if masked:
        col = lax.broadcasted_iota(jnp.int32, (QBLK, keys), 1) // MROWS
        allowed = jnp.zeros((QBLK, keys), jnp.bool_)
    for s, (kr, vr) in enumerate(((k0, v0), (k1, v1), (k2, v2), (k3, v3))):
        for r in range(CAP):
            n = s * CAP + r
            entry = info[slot, n]
            start = pl.multiple_of(jnp.maximum(entry, 0) * MROWS, MROWS)
            kbuf[n * MROWS : (n + 1) * MROWS, :] = kr[pl.ds(start, MROWS), :]
            vbuf[n * MROWS : (n + 1) * MROWS, :] = vr[pl.ds(start, MROWS), :]
            if masked:
                allowed = allowed | ((col == n) & (entry >= 0))
    rows = attend_heads(q_ref[0], kbuf[...], vbuf[...], allowed, out_ref, jnp.zeros((QBLK, HD), jnp.float32))
    lse_ref[0, 0, :G] = rows.T[:G]
    lse_ref[0, 0, G:] = ctx_lse_ref[0, 0, :G]


def scale_kernel(planes, info, um_ref, uc_ref, gate_ref, *rest):
    lse_refs, out_ref = rest[:-1], rest[-1]
    slot = pl.program_id(1)
    own = info[planes, slot]
    parts = [lse_refs[k][info[k, slot], 0] for k in range(planes)]
    top = functools.reduce(jnp.maximum, parts)
    total = functools.reduce(jnp.add, [jnp.exp2(p - top) for p in parts])
    mine = lse_refs[0][own, 0] if planes == WITHIN else parts[0]
    if planes != WITHIN:
        for k in range(1, planes):
            mine = jnp.where(info[planes + 1, 0] == k, parts[k], mine)
    weight = jnp.exp2(mine - top) / total * gate_ref[0]
    wt = jnp.concatenate([weight, jnp.zeros((HD - 8, QBLK), jnp.float32)], axis=0).T
    for g in range(G):
        cols = slice(g * HD, (g + 1) * HD)
        mixed = wt[:, g : g + 1] * um_ref[0, :, cols].astype(jnp.float32)
        mixed += wt[:, G + g : G + g + 1] * uc_ref[0, :, cols].astype(jnp.float32)
        out_ref[0, :, cols] = mixed.astype(jnp.bfloat16)


def cost(tiles, rows_bytes):
    return pl.CostEstimate(
        flops=tiles * 2 * 1024 * 1024 * 128 * 2, bytes_accessed=rows_bytes, transcendentals=tiles * 1024 * 1024
    )


PARAMS = pltpu.CompilerParams(vmem_limit_bytes=48 * 1024 * 1024)


def ctx_call(info, q, sources, first, count):
    planes = q.shape[0]
    kspec = pl.BlockSpec((QBLK, HD), lambda h, j, info: (0, first + h))
    vspec = pl.BlockSpec((QBLK, HD), lambda h, j, info: (0, KVH + first + h))
    block = pl.BlockSpec((1, QBLK, QW), lambda h, j, info: (j, 0, h))
    return pl.pallas_call(
        ctx_kernel,
        grid_spec=pltpu.PrefetchScalarGridSpec(
            num_scalar_prefetch=1,
            grid=(count, planes),
            in_specs=[block] + [kspec] * WITHIN + [vspec] * WITHIN,
            out_specs=[block, pl.BlockSpec((1, 1, 8, QBLK), lambda h, j, info: (j, h, 0, 0))],
        ),
        out_shape=[
            jax.ShapeDtypeStruct(q.shape, jnp.bfloat16),
            jax.ShapeDtypeStruct((planes, count, 8, QBLK), jnp.float32),
        ],
        compiler_params=PARAMS,
        cost_estimate=cost(count * planes, 4 * 1024 * 1024),
        name="ctx_attend",
    )(info, q, *sources, *sources)


def mem_call(info, q, wide, narrow, ctx_lse, first, count, masked):
    planes = q.shape[0]
    rows = wide[0].shape[0]
    wspec = pl.BlockSpec((rows, HD), lambda h, j, info: (0, first + h))
    kspec = pl.BlockSpec((rows, HD), lambda h, j, info: (0, h))
    vspec = pl.BlockSpec((rows, HD), lambda h, j, info: (0, count + h))
    block = pl.BlockSpec((1, QBLK, QW), lambda h, j, info: (j, 0, h))
    lse = pl.BlockSpec((1, 1, 8, QBLK), lambda h, j, info: (j, h, 0, 0))
    own_k, own_v, near_k, near_v = wide
    far, diag = narrow
    keys = WITHIN * CAP * MROWS
    return pl.pallas_call(
        functools.partial(mem_kernel, masked),
        grid_spec=pltpu.PrefetchScalarGridSpec(
            num_scalar_prefetch=1,
            grid=(count, planes),
            in_specs=[block, wspec, wspec, kspec, kspec, wspec, wspec, vspec, vspec, lse],
            out_specs=[block, lse],
            scratch_shapes=[pltpu.VMEM((keys, HD), jnp.bfloat16), pltpu.VMEM((keys, HD), jnp.bfloat16)],
        ),
        out_shape=[
            jax.ShapeDtypeStruct(q.shape, jnp.bfloat16),
            jax.ShapeDtypeStruct((planes, count, 8, QBLK), jnp.float32),
        ],
        compiler_params=PARAMS,
        cost_estimate=cost(count * planes, 4 * 1024 * 1024),
        name="mem_attend",
    )(info, q, own_k, near_k, far, diag, own_v, near_v, far, diag, ctx_lse)


def scale_call(info, um, uc, gate_rows, lses):
    planes, _, width = um.shape
    count = width // QW
    block = pl.BlockSpec((1, QBLK, QW), lambda h, j, info: (j, 0, h))
    lse = pl.BlockSpec((planes, 1, 8, QBLK), lambda h, j, info: (0, h, 0, 0))
    return pl.pallas_call(
        functools.partial(scale_kernel, planes),
        grid_spec=pltpu.PrefetchScalarGridSpec(
            num_scalar_prefetch=1,
            grid=(count, planes),
            in_specs=[block, block, pl.BlockSpec((1, 8, 1), lambda h, j, info: (h, 0, 0))] + [lse] * planes,
            out_specs=block,
        ),
        out_shape=jax.ShapeDtypeStruct(um.shape, jnp.bfloat16),
        compiler_params=PARAMS,
        cost_estimate=pl.CostEstimate(flops=8 * um.size, bytes_accessed=6 * um.size, transcendentals=0),
        name="scale_mix",
    )(info, um, uc, gate_rows, *lses)


def on_device(
    queries, ctx_keys, ctx_values, store_keys, store_values, block_ids, block_slot, gate_logit
):
    devices = lax.axis_size("seq")
    planes = devices // WITHIN
    chain = planes == WITHIN
    me = lax.axis_index("seq")
    plane, within = me // WITHIN, me % WITHIN
    local_count = store_keys.shape[0]
    masked = devices * CAP != TOPM

    def move(x, pairs):
        return lax.ppermute(x, "seq", pairs)

    def xor(x, bits):
        return move(x, [(i, i ^ bits) for i in range(devices)])

    def between(x, plane_pairs):
        return move(x, [(a * WITHIN + w, b * WITHIN + w) for a, b in plane_pairs for w in range(WITHIN)])

    columns = [[p * WITHIN + w for p in range(planes)] for w in range(WITHIN)]

    def gather_planes(x):
        return lax.all_gather(x, "seq", axis=0, axis_index_groups=columns)

    keys = store_keys.reshape(local_count * MROWS, KVH * HD)
    values = store_values.reshape(local_count * MROWS, KVH * HD)

    def store_part(first, count):
        cols = slice(first * HD, (first + count) * HD)
        return jnp.concatenate([keys[:, cols], values[:, cols]], axis=1)

    ctx_own = jnp.concatenate([ctx_keys, ctx_values], axis=1)

    table = request_table(lookup_slots(block_ids.reshape(-1), block_slot), devices, local_count)

    if chain:
        inner = (plane == 1) | (plane == 2)
        low = jnp.where(inner, 3, 2)

        def place(p, target):
            x = p ^ target
            p_inner = (p == 1) | (p == 2)
            return jnp.where(p_inner & (x >= 2), 5 - x, x)

        slot_plane = jnp.stack([plane, plane ^ 1, plane ^ low, plane ^ (5 - low)])
        tables = [table, xor(table, 4), xor(table, 8), xor(table, 12)]
        far_a = jnp.where(inner, tables[3], tables[2])
        far_b = jnp.where(inner, tables[2], tables[3])
        tables = jnp.stack([tables[0], tables[1], far_a, far_b])
        lse_index = jnp.stack([place(plane ^ k, slot_plane) for k in range(planes)] + [jnp.arange(planes)])
    else:
        slot_plane = jnp.arange(planes, dtype=jnp.int32)
        tables = gather_planes(table)
        steps = jnp.arange(planes, dtype=jnp.int32)
        lse_index = jnp.concatenate(
            [jnp.broadcast_to(steps, (planes + 1, planes)), jnp.broadcast_to(plane, (1, planes))]
        )
    lse_index = lse_index.astype(jnp.int32)
    wanted = lax.dynamic_slice_in_dim(tables, plane * WITHIN, WITHIN, 1)
    wanted = jnp.stack([jnp.take(wanted, within ^ s, axis=1) for s in range(WITHIN)], axis=1)
    wanted = wanted.reshape(planes, WITHIN * CAP).astype(jnp.int32)
    ctx_info = jnp.concatenate([jnp.stack([plane, within]), slot_plane]).astype(jnp.int32)

    gate = 1.0 / (1.0 + jnp.exp(-gate_logit))
    gate_rows = jnp.concatenate([gate.reshape(KVH, G), 1.0 - gate.reshape(KVH, G)], axis=1)[:, :, None]

    def spread_queries(part):
        if not chain:
            return gather_planes(part)
        near = xor(part, 4)
        pair = jnp.stack([part, near])
        crossed = between(pair, [(1, 2), (2, 1)])
        handed = between(crossed, [(1, 0), (2, 3)])
        far = jnp.where(inner, crossed, handed)
        return jnp.concatenate([pair, far], axis=0)

    def collect(parts):
        if not chain:
            return lax.psum_scatter(parts, "seq", scatter_dimension=0, axis_index_groups=columns)
        handed = between(parts[2:], [(0, 1), (3, 2)])
        crossed = between(
            (parts[2:].astype(jnp.float32) + handed.astype(jnp.float32)).astype(jnp.bfloat16), [(1, 2), (2, 1)]
        )
        pair = parts[:2].astype(jnp.float32) + crossed.astype(jnp.float32)
        near = xor(pair[1].astype(jnp.bfloat16), 4)
        return (pair[0] + near.astype(jnp.float32)).astype(jnp.bfloat16)

    far_stores = [xor(store_part(first, count), 2) for first, count in STAGES[:1]]
    ctx_far = xor(ctx_own, 2)
    far_stores += [xor(store_part(first, count), 2) for first, count in STAGES[1:]]
    near_keys, near_values = xor(keys, 1), xor(values, 1)
    ctx_near = xor(ctx_own, 1)
    ctx_diag = xor(ctx_far, 1)
    wide = (keys, values, near_keys, near_values)

    results = []
    for (first, count), far in zip(STAGES, far_stores, strict=True):
        q = spread_queries(queries[:, first * QW : (first + count) * QW])
        uc, ctx_lse = ctx_call(ctx_info, q, (ctx_own, ctx_near, ctx_far, ctx_diag), first, count)
        um, lse = mem_call(wanted, q, wide, (far, xor(far, 1)), ctx_lse, first, count, masked)
        if chain:
            lses = [lse, xor(lse, 4), xor(lse, 8), xor(lse, 12)]
        else:
            every = gather_planes(lse)
            lses = [every[k] for k in range(planes)]
        parts = scale_call(lse_index, um, uc, gate_rows[first : first + count], lses)
        results.append(collect(parts))
    return jnp.concatenate(results, axis=1)


def solution(mesh):
    placed = (
        P(("groups", "seq"), None),
        P(("groups", "seq"), None),
        P(("groups", "seq"), None),
        P(("groups", "seq"), None, None),
        P(("groups", "seq"), None, None),
        P(("groups", "seq"), None),
        P("groups"),
        P(),
    )
    return jax.shard_map(
        on_device, mesh=mesh, in_specs=placed, out_specs=P(("groups", "seq"), None), check_vma=False
    )
```

```python
import functools

import jax
import jax.numpy as jnp
from jax import lax
from jax.experimental import pallas as pl
from jax.experimental.pallas import tpu as pltpu
from jax.sharding import PartitionSpec as P

H = 16
KVH = 4
HD = 128
QBLK = 256
MROWS = 128
TOPM = 32
CAP = 2
G = H // KVH
WITHIN = 4
LOG2E = 1.4426950408889634
SCALE = HD**-0.5 * LOG2E
MASKED = -1e30
QW = G * HD
QUERY_PLAN = (((0,), "direct"), ((1,), "gather"), ((2, 3), "gather"))
GROUPS = (((0, 1), "scatter"), ((2,), "direct"), ((3,), "direct"))


def wanted_blocks(slots, plane, within, local_count):
    owner = (slots // local_count)[:, None, :]
    holder = plane * WITHIN + (within ^ jnp.arange(WITHIN, dtype=jnp.int32))
    hits = (owner == holder[None, :, None]).astype(jnp.int32)
    rank = jnp.cumsum(hits, axis=2) * hits
    local = (slots % local_count + 1)[:, None, :]
    picked = [jnp.sum(jnp.where(rank == r + 1, local, 0), axis=2) - 1 for r in range(CAP)]
    return jnp.stack(picked, axis=2).reshape(slots.shape[0], WITHIN * CAP)


def lookup_slots(wanted_ids, block_slot):
    hits = wanted_ids[..., None] == jnp.arange(block_slot.shape[0], dtype=jnp.int32)
    return jnp.sum(jnp.where(hits, block_slot, 0), axis=-1)


def scores_of(q, k):
    return lax.dot_general(q, k, (((1,), (1,)), ((), ())), preferred_element_type=jnp.float32)


def attend_heads(q, k, v, allowed, out_ref):
    keys = k.shape[0]
    vx = jnp.concatenate([v, jnp.ones((keys, HD), jnp.bfloat16)], axis=1)
    lane = lax.broadcasted_iota(jnp.int32, (QBLK, HD), 1)
    rows = jnp.zeros((QBLK, HD), jnp.float32)
    ahead = scores_of(q[:, :HD], k)
    for g in range(G):
        s = ahead
        if g + 1 < G:
            ahead = scores_of(q[:, (g + 1) * HD : (g + 2) * HD], k)
        if allowed is not None:
            s = jnp.where(allowed, s, MASKED)
        m = jnp.max(s, axis=1, keepdims=True)
        p = jnp.exp2((s - m) * SCALE).astype(jnp.bfloat16)
        o = jnp.dot(p, vx, preferred_element_type=jnp.float32)
        total = o[:, HD:]
        out_ref[0, :, g * HD : (g + 1) * HD] = (o[:, :HD] / total).astype(jnp.bfloat16)
        rows = jnp.where(lane == g, m * SCALE + jnp.log2(total), rows)
    return rows.T[:8]


def pick_query(slot, q_refs, qbuf):
    if len(q_refs) == 1:
        return q_refs[0][0]
    for i, ref in enumerate(q_refs):

        @pl.when(slot == i)
        def _(ref=ref):
            qbuf[...] = ref[...]

    return qbuf[...]


def ctx_kernel(n_q, info, *refs):
    q_refs = refs[:n_q]
    k0, k1, k2, k3, v0, v1, v2, v3, out_ref, lse_ref, qbuf = refs[n_q:]
    slot = pl.program_id(1)
    plane, within = info[0, 0], info[0, 1]
    target = jnp.bitwise_xor(plane, slot)

    def run(allowed):
        k = jnp.concatenate([k0[...], k1[...], k2[...], k3[...]], axis=0)
        v = jnp.concatenate([v0[...], v1[...], v2[...], v3[...]], axis=0)
        lse_ref[0, 0] = attend_heads(pick_query(slot, q_refs, qbuf), k, v, allowed, out_ref.at[0])

    @pl.when(target > plane)
    def _():
        run(None)

    @pl.when(target == plane)
    def _():
        keys = WITHIN * QBLK
        col = lax.broadcasted_iota(jnp.int32, (QBLK, keys), 1)
        row = lax.broadcasted_iota(jnp.int32, (QBLK, keys), 0)
        key_pos = jnp.bitwise_xor(col // QBLK, within) * QBLK + col % QBLK
        run(key_pos <= within * QBLK + row)

    @pl.when(target < plane)
    def _():
        out_ref[...] = jnp.zeros_like(out_ref)
        lse_ref[...] = jnp.full_like(lse_ref, MASKED)


def mem_kernel(masked, n_q, info, *refs):
    q_refs = refs[:n_q]
    stores = refs[n_q : n_q + WITHIN]
    ctx_lse_ref, out_ref, lse_ref, kbuf, vbuf, qbuf = refs[n_q + WITHIN :]
    slot = pl.program_id(0)
    allowed = None
    keys = WITHIN * CAP * MROWS
    if masked:
        col = lax.broadcasted_iota(jnp.int32, (QBLK, keys), 1) // MROWS
        allowed = jnp.zeros((QBLK, keys), jnp.bool_)
    for n in range(WITHIN * CAP):
        entry = info[1 + slot, n]
        start = pl.multiple_of(jnp.maximum(entry, 0) * MROWS, MROWS)
        rows, to = pl.ds(start, MROWS), slice(n * MROWS, (n + 1) * MROWS)
        kbuf[to, :] = stores[n // CAP][0, rows, :]
        vbuf[to, :] = stores[n // CAP][1, rows, :]
        if masked:
            allowed = allowed | ((col == n) & (entry >= 0))
    query = pick_query(slot, q_refs, qbuf)
    lse_ref[0] = attend_heads(query, kbuf[...], vbuf[...], allowed, out_ref)
    lse_ref[0, G:] = ctx_lse_ref[0, 0, :G]


def scale_kernel(planes, heads, info, *refs):
    um_refs, uc_refs, gate_ref = refs[:heads], refs[heads : 2 * heads], refs[2 * heads]
    lse_refs, out_refs = refs[2 * heads + 1 : 2 * heads + 1 + planes], refs[2 * heads + 1 + planes :]
    slot = pl.program_id(0)
    for h in range(heads):
        parts = [lse_refs[k][h, jnp.bitwise_xor(slot, k)] for k in range(planes)]
        top = functools.reduce(jnp.maximum, parts)
        total = functools.reduce(jnp.add, [jnp.exp2(p - top) for p in parts])
        weight = jnp.exp2(parts[0] - top) / total * gate_ref[h]
        wt = jnp.concatenate([weight, jnp.zeros((HD - 8, QBLK), jnp.float32)], axis=0).T
        for g in range(G):
            cols = slice(g * HD, (g + 1) * HD)
            term = wt[:, g : g + 1] * um_refs[h][0, :, cols].astype(jnp.float32)
            term += wt[:, G + g : G + g + 1] * uc_refs[h][0, 0, :, cols].astype(jnp.float32)
            term = term.astype(jnp.bfloat16)
            if len(out_refs) == 1:
                out_refs[0][0, h, :, cols] = term
                continue
            for i, ref in enumerate(out_refs):

                @pl.when(slot == i)
                def _(ref=ref):
                    ref[h, :, cols] = term


PARAMS = pltpu.CompilerParams(vmem_limit_bytes=20 * 1024 * 1024)
PACK_PARAMS = pltpu.CompilerParams(vmem_limit_bytes=60 * 1024 * 1024)
SMALL = pl.CostEstimate(flops=1000, bytes_accessed=1000, transcendentals=0)


def query_place(head):
    return next((n, heads.index(head)) for n, (heads, _) in enumerate(QUERY_PLAN) if head in heads)


def whole(shape):
    return pl.BlockSpec(shape, lambda *_: (0,) * len(shape))


def query_specs(qs, chosen):
    if len(qs) == 1:
        return [pl.BlockSpec((1, QBLK, QW), lambda *i: (jnp.bitwise_xor(i[-1][0, 0], i[-2]), 0, chosen(*i)))]
    return [pl.BlockSpec((QBLK, QW), lambda *i: (0, chosen(*i)))] * len(qs)


def ctx_call(info, qs, sources, first, count, planes):
    kspec = pl.BlockSpec((QBLK, HD), lambda h, j, info: (0, first + h))
    vspec = pl.BlockSpec((QBLK, HD), lambda h, j, info: (0, KVH + first + h))
    return pl.pallas_call(
        functools.partial(ctx_kernel, len(qs)),
        grid_spec=pltpu.PrefetchScalarGridSpec(
            num_scalar_prefetch=1,
            grid=(count, planes),
            in_specs=query_specs(qs, lambda h, j, info: query_place(first)[1] + h) + [kspec] * WITHIN + [vspec] * WITHIN,
            out_specs=[
                pl.BlockSpec((1, 1, QBLK, QW), lambda h, j, info: (h, j, 0, 0)),
                pl.BlockSpec((1, 1, 8, QBLK), lambda h, j, info: (h, j, 0, 0)),
            ],
            scratch_shapes=[pltpu.VMEM((QBLK, QW), jnp.bfloat16)],
        ),
        out_shape=[
            jax.ShapeDtypeStruct((count, planes, QBLK, QW), jnp.bfloat16),
            jax.ShapeDtypeStruct((count, planes, 8, QBLK), jnp.float32),
        ],
        compiler_params=PARAMS,
        cost_estimate=SMALL,
        name="ctx_attend",
    )(info, *qs, *sources, *sources)


def mem_call(info, qs, stores, ctx_lse, head, nth, planes, masked):
    keys = WITHIN * CAP * MROWS
    return pl.pallas_call(
        functools.partial(mem_kernel, masked, len(qs)),
        grid_spec=pltpu.PrefetchScalarGridSpec(
            num_scalar_prefetch=1,
            grid=(planes,),
            in_specs=query_specs(qs, lambda j, info: query_place(head)[1])
            + [whole(stores[0].shape)] * WITHIN
            + [pl.BlockSpec((1, 1, 8, QBLK), lambda j, info: (nth, j, 0, 0))],
            out_specs=[
                pl.BlockSpec((1, QBLK, QW), lambda j, info: (j, 0, 0)),
                pl.BlockSpec((1, 8, QBLK), lambda j, info: (j, 0, 0)),
            ],
            scratch_shapes=[
                pltpu.VMEM((keys, HD), jnp.bfloat16),
                pltpu.VMEM((keys, HD), jnp.bfloat16),
                pltpu.VMEM((QBLK, QW), jnp.bfloat16),
            ],
        ),
        out_shape=[
            jax.ShapeDtypeStruct((planes, QBLK, QW), jnp.bfloat16),
            jax.ShapeDtypeStruct((planes, 8, QBLK), jnp.float32),
        ],
        compiler_params=PARAMS,
        cost_estimate=SMALL,
        name="mem_attend",
    )(info, *qs, *stores, ctx_lse)


def scale_call(info, ums, ucs, gate_rows, lses, apart):
    heads, planes = len(ums), ums[0].shape[0]
    if apart:
        out_specs = [whole((heads, QBLK, QW))] * planes
        out_shape = [jax.ShapeDtypeStruct((heads, QBLK, QW), jnp.bfloat16)] * planes
    else:
        out_specs = [pl.BlockSpec((1, heads, QBLK, QW), lambda j, info: (jnp.bitwise_xor(info[0, 0], j), 0, 0, 0))]
        out_shape = [jax.ShapeDtypeStruct((planes, heads, QBLK, QW), jnp.bfloat16)]
    return pl.pallas_call(
        functools.partial(scale_kernel, planes, heads),
        grid_spec=pltpu.PrefetchScalarGridSpec(
            num_scalar_prefetch=1,
            grid=(planes,),
            in_specs=[pl.BlockSpec((1, QBLK, QW), lambda j, info: (j, 0, 0))] * heads
            + [pl.BlockSpec((1, 1, QBLK, QW), lambda j, info: (0, j, 0, 0))] * heads
            + [whole((heads, 8, 1))]
            + [whole((heads, planes, 8, QBLK))] * planes,
            out_specs=out_specs,
        ),
        out_shape=out_shape,
        compiler_params=PARAMS,
        cost_estimate=SMALL,
        name="scale_mix",
    )(info, *ums, *ucs, gate_rows, *lses)


def pack_kernel(heads, with_ctx, q, ck, cv, k, v, *outs):
    for n, head in enumerate(heads):
        cols = slice(head * HD, (head + 1) * HD)
        outs[n][0] = k[:, cols]
        outs[n][1] = v[:, cols]
    if with_ctx:
        for n, (chunk, _) in enumerate(QUERY_PLAN):
            outs[len(heads) + n][...] = q[:, chunk[0] * QW : (chunk[-1] + 1) * QW]
        outs[-1][:, : KVH * HD] = ck[...]
        outs[-1][:, KVH * HD :] = cv[...]


def pack_call(heads, with_ctx, q, ck, cv, k, v):
    rows, steps = k.shape[0], 4
    wide = len(heads) > 1
    part, piece = rows // steps, q.shape[0] // steps

    def row_block(r, c):
        return pl.BlockSpec((r, c), lambda i: (i, 0))

    shapes, specs = [], []
    for _ in heads:
        shapes.append(jax.ShapeDtypeStruct((2, rows, HD), jnp.bfloat16))
        specs.append(pl.BlockSpec((2, part, HD), lambda i: (0, i, 0)))
    if with_ctx:
        for chunk, _ in QUERY_PLAN:
            shapes.append(jax.ShapeDtypeStruct((q.shape[0], len(chunk) * QW), jnp.bfloat16))
            specs.append(row_block(piece, len(chunk) * QW))
        shapes.append(jax.ShapeDtypeStruct((ck.shape[0], 2 * KVH * HD), jnp.bfloat16))
        specs.append(row_block(piece, 2 * KVH * HD))
    ctx = row_block(piece, KVH * HD)
    store = row_block(part, (KVH if wide else 1) * HD)
    return pl.pallas_call(
        functools.partial(pack_kernel, heads, with_ctx),
        grid=(steps,),
        in_specs=[row_block(piece, KVH * QW), ctx, ctx, store, store],
        out_specs=specs,
        out_shape=shapes,
        compiler_params=PACK_PARAMS,
        cost_estimate=SMALL,
        name="pack_heads",
    )(q, ck, cv, k, v)


class Order:
    def __init__(self):
        self.last = ()

    def before(self, *arrays):
        if not self.last:
            return arrays
        return lax.optimization_barrier((*arrays, *self.last))[: len(arrays)]

    def done(self, *arrays):
        self.last = arrays


def on_device(
    queries, ctx_keys, ctx_values, store_keys, store_values, block_ids, block_slot, gate_logit
):
    devices = lax.axis_size("seq")
    planes = devices // WITHIN
    me = lax.axis_index("seq")
    plane, within = me // WITHIN, me % WITHIN
    local_count = store_keys.shape[0]
    masked = devices * CAP != TOPM

    def xor(x, bits):
        return lax.ppermute(x, "seq", [(i, i ^ bits) for i in range(devices)])

    def all_planes(x):
        return [x] + [xor(x, k * WITHIN) for k in range(1, planes)]

    columns = [[p * WITHIN + w for p in range(planes)] for w in range(WITHIN)]
    keys = store_keys.reshape(local_count * MROWS, KVH * HD)
    values = store_values.reshape(local_count * MROWS, KVH * HD)
    order = Order()

    ids = all_planes(block_ids.reshape(-1))
    kv, *q_chunks, ctx_own = pack_call((0,), True, queries, ctx_keys, ctx_values, keys, values)
    ctx_far = xor(ctx_own, 2)
    own = [kv]
    far = [xor(kv, 2)]
    order.done(ctx_own, *ids)
    own += pack_call((1, 2, 3), False, *order.before(queries, ctx_keys, ctx_values, keys, values))
    order.done(own[1])
    far += [xor(part, 2) for part in own[1:]]
    ctx_near = xor(ctx_own, 1)
    near = [xor(part, 1) for part in own]
    ctx_diag = xor(ctx_far, 1)

    wanted = wanted_blocks(lookup_slots(jnp.stack(ids), block_slot), plane, within, local_count)
    info = jnp.concatenate([jnp.stack([plane, within] + [plane] * 6)[None], wanted]).astype(jnp.int32)

    gate = 1.0 / (1.0 + jnp.exp(-gate_logit))
    gate_rows = jnp.concatenate([gate.reshape(KVH, G), 1.0 - gate.reshape(KVH, G)], axis=1)[:, :, None]

    def spread_queries(part, how):
        if how == "direct":
            return all_planes(part)
        return [lax.all_gather(part, "seq", axis=0, axis_index_groups=columns)]

    spread = [spread_queries(part, how) for part, (_, how) in zip(q_chunks, QUERY_PLAN, strict=True)]
    sources = (ctx_own, ctx_near, ctx_far, ctx_diag)
    diag = [None] * KVH

    def fetch_step(head):
        (far[head],) = order.before(far[head])
        order.done(far[head])
        diag[head] = xor(far[head], 1)

    def ctx_step(first, count):
        qs = spread[query_place(first)[0]]
        args = order.before(info, *qs, *sources)
        n = len(qs) + 1
        uc, lse = ctx_call(args[0], args[1:n], args[n:], first, count, planes)
        order.done(lse)
        return uc, lse

    def mem_step(head, ctx_lse):
        qs = spread[query_place(head)[0]]
        args = order.before(info, *qs, own[head], near[head], far[head], diag[head], ctx_lse)
        n = len(qs) + 1
        um, lse = mem_call(args[0], args[1:n], args[n : n + WITHIN], args[n + WITHIN], head, 0, planes, masked)
        order.done(lse)
        return um, lse

    def exchange(parts):
        return all_planes(jnp.stack([lse for _, lse in parts]))

    def scale_step(nth, ums, ucs, lses):
        group, how = GROUPS[nth]
        n, m = len(ums), len(ums) + len(ucs)
        args = order.before(*ums, *ucs, *lses)
        gates = gate_rows[group[0] : group[-1] + 1]
        parts = scale_call(info, args[:n], args[n:m], gates, args[m:], how == "direct")
        order.done(*parts[:1])
        if how == "direct":
            return [parts[0]] + [xor(parts[k], k * WITHIN) for k in range(1, planes)]
        return [lax.psum_scatter(parts[0], "seq", scatter_dimension=0, axis_index_groups=columns)]

    def total(parts):
        return sum(part.astype(jnp.float32) for part in parts).astype(jnp.bfloat16)

    fetch_step(0)
    uc0, ctx_lse0 = ctx_step(0, 1)
    mem0 = mem_step(0, ctx_lse0)
    fetch_step(1)
    uc1, ctx_lse1 = ctx_step(1, 1)
    mem1 = mem_step(1, ctx_lse1)
    lses = exchange([mem0, mem1])
    fetch_step(2)
    uc2, ctx_lse2 = ctx_step(2, 1)
    coming = [scale_step(0, [mem0[0], mem1[0]], [uc0, uc1], lses)]
    mem2 = mem_step(2, ctx_lse2)
    lses = exchange([mem2])
    fetch_step(3)
    uc3, ctx_lse3 = ctx_step(3, 1)
    coming.append(scale_step(1, [mem2[0]], [uc2], lses))
    mem3 = mem_step(3, ctx_lse3)
    coming.append(scale_step(2, [mem3[0]], [uc3], exchange([mem3])))
    return jnp.concatenate([part for parts in coming for part in total(parts)], axis=1)


def solution(mesh):
    placed = (
        P(("groups", "seq"), None),
        P(("groups", "seq"), None),
        P(("groups", "seq"), None),
        P(("groups", "seq"), None, None),
        P(("groups", "seq"), None, None),
        P(("groups", "seq"), None),
        P("groups"),
        P(),
    )
    return jax.shard_map(
        on_device, mesh=mesh, in_specs=placed, out_specs=P(("groups", "seq"), None), check_vma=False
    )
```

```python
import functools

import jax
import jax.numpy as jnp
from jax import lax
from jax.experimental import pallas as pl
from jax.experimental.pallas import tpu as pltpu
from jax.sharding import PartitionSpec as P

H = 16
KVH = 4
HD = 128
QBLK = 256
MROWS = 128
TOPM = 32
CAP = 2
G = H // KVH
WITHIN = 4
LOG2E = 1.4426950408889634
SCALE = HD**-0.5 * LOG2E
MASKED = -1e30
QW = G * HD
CHUNKS = ((0, 1), (2, 3))
ID_ROWS = 16
GROUPS = (((0, 1), "scatter"), ((2,), "direct"), ((3,), "direct"))


def scores_of(q, k):
    return lax.dot_general(q, k, (((1,), (1,)), ((), ())), preferred_element_type=jnp.float32)


def attend_heads(q, k, v, allowed, out_ref):
    keys = k.shape[0]
    vx = jnp.concatenate([v, jnp.ones((keys, HD), jnp.bfloat16)], axis=1)
    lane = lax.broadcasted_iota(jnp.int32, (QBLK, HD), 1)
    rows = jnp.zeros((QBLK, HD), jnp.float32)
    ahead = scores_of(q[:, :HD], k)
    for g in range(G):
        s = ahead
        if g + 1 < G:
            ahead = scores_of(q[:, (g + 1) * HD : (g + 2) * HD], k)
        if allowed is not None:
            s = jnp.where(allowed, s, MASKED)
        m = jnp.max(s, axis=1, keepdims=True)
        p = jnp.exp2((s - m) * SCALE).astype(jnp.bfloat16)
        o = jnp.dot(p, vx, preferred_element_type=jnp.float32)
        total = o[:, HD:]
        out_ref[0, :, g * HD : (g + 1) * HD] = (o[:, :HD] / total).astype(jnp.bfloat16)
        rows = jnp.where(lane == g, m * SCALE + jnp.log2(total), rows)
    return rows.T[:8]


def ctx_kernel(slot_base, info, q_ref, k0, k1, k2, k3, v0, v1, v2, v3, out_ref, lse_ref):
    slot = pl.program_id(1) + slot_base
    plane, within = info[0, 0], info[0, 1]
    target = jnp.bitwise_xor(plane, slot)

    def run(allowed):
        k = jnp.concatenate([k0[...], k1[...], k2[...], k3[...]], axis=0)
        v = jnp.concatenate([v0[...], v1[...], v2[...], v3[...]], axis=0)
        lse_ref[0, 0] = attend_heads(q_ref[0] if slot_base else q_ref[...], k, v, allowed, out_ref.at[0])

    if slot_base == 0:
        keys = WITHIN * QBLK
        col = lax.broadcasted_iota(jnp.int32, (QBLK, keys), 1)
        row = lax.broadcasted_iota(jnp.int32, (QBLK, keys), 0)
        key_pos = jnp.bitwise_xor(col // QBLK, within) * QBLK + col % QBLK
        run(key_pos <= within * QBLK + row)
        return

    @pl.when(target > plane)
    def _():
        run(None)

    @pl.when(target < plane)
    def _():
        out_ref[...] = jnp.zeros_like(out_ref)
        lse_ref[...] = jnp.full_like(lse_ref, MASKED)


def mem_kernel(masked, info, q_ref, s0, s1, s2, s3, own_lse_ref, ctx_lse_ref, out_ref, lse_ref, kbuf, vbuf):
    slot = pl.program_id(1)
    stores = (s0, s1, s2, s3)
    allowed = None
    keys = WITHIN * CAP * MROWS
    if masked:
        col = lax.broadcasted_iota(jnp.int32, (QBLK, keys), 1) // MROWS
        allowed = jnp.zeros((QBLK, keys), jnp.bool_)
    for n in range(WITHIN * CAP):
        entry = info[1 + slot, n]
        start = pl.multiple_of(jnp.maximum(entry, 0) * MROWS, MROWS)
        rows, to = pl.ds(start, MROWS), slice(n * MROWS, (n + 1) * MROWS)
        kbuf[to, :] = stores[n // CAP][rows, :HD]
        vbuf[to, :] = stores[n // CAP][rows, HD:]
        if masked:
            allowed = allowed | ((col == n) & (entry >= 0))
    lse_ref[0, 0] = attend_heads(q_ref[0], kbuf[...], vbuf[...], allowed, out_ref.at[0])
    lse_ref[0, 0, G:] = jnp.where(slot == 0, own_lse_ref[0, 0, :G], ctx_lse_ref[0, 0, :G])


def scale_kernel(planes, heads, scattered, info, um_ref, own_ref, uc_ref, gate_ref, *refs):
    lse_refs, out_refs = refs[:planes], refs[planes:]
    slot = pl.program_id(0)
    for h in range(heads):
        parts = [lse_refs[k][h, jnp.bitwise_xor(slot, k)] for k in range(planes)]
        top = functools.reduce(jnp.maximum, parts)
        total = functools.reduce(jnp.add, [jnp.exp2(p - top) for p in parts])
        weight = jnp.exp2(parts[0] - top) / total * gate_ref[h]
        wt = jnp.concatenate([weight, jnp.zeros((HD - 8, QBLK), jnp.float32)], axis=0).T
        for g in range(G):
            cols = slice(g * HD, (g + 1) * HD)
            term = wt[:, g : g + 1] * um_ref[h, 0, :, cols].astype(jnp.float32)
            ctx = jnp.where(slot == 0, own_ref[h, 0, :, cols], uc_ref[h, 0, :, cols])
            term += wt[:, G + g : G + g + 1] * ctx.astype(jnp.float32)
            term = term.astype(jnp.bfloat16)
            if scattered:
                out_refs[0][0, h, :, cols] = term
                continue
            for i, ref in enumerate(out_refs):

                @pl.when(slot == i)
                def _(ref=ref):
                    ref[h, :, cols] = term


PARAMS = pltpu.CompilerParams(vmem_limit_bytes=56 * 1024 * 1024)
PACK_PARAMS = pltpu.CompilerParams(vmem_limit_bytes=60 * 1024 * 1024)
SMALL = pl.CostEstimate(flops=1000, bytes_accessed=1000, transcendentals=0)


def place_of(head, chunks):
    return next((n, heads.index(head)) for n, heads in enumerate(chunks) if head in heads)


def whole(shape):
    return pl.BlockSpec(shape, lambda *_: (0,) * len(shape))


def query_spec(first):
    column = place_of(first, CHUNKS)[1]
    return pl.BlockSpec((1, QBLK, QW), lambda h, j, info: (jnp.bitwise_xor(info[0, 0], j), 0, column + h))


def per_head(rows, cols):
    return pl.BlockSpec((1, 1, rows, cols), lambda h, j, info: (h, j, 0, 0))


def partial_shapes(count, planes):
    return [
        jax.ShapeDtypeStruct((count, planes, QBLK, QW), jnp.bfloat16),
        jax.ShapeDtypeStruct((count, planes, 8, QBLK), jnp.float32),
    ]


def ctx_call(info, q, sources, first, count, planes):
    base = min(planes - 1, 1)
    kspec = pl.BlockSpec((QBLK, HD), lambda h, j, info: (0, first + h))
    if base:
        column = place_of(first, CHUNKS)[1]
        qspec = pl.BlockSpec((1, QBLK, QW), lambda h, j, info: (jnp.bitwise_xor(info[0, 0], j + 1), 0, column + h))
    else:
        qspec = pl.BlockSpec((QBLK, QW), lambda h, j, info: (0, first + h))
    return pl.pallas_call(
        functools.partial(ctx_kernel, base),
        grid_spec=pltpu.PrefetchScalarGridSpec(
            num_scalar_prefetch=1,
            grid=(count, planes - base),
            in_specs=[qspec] + [kspec] * (2 * WITHIN),
            out_specs=[per_head(QBLK, QW), per_head(8, QBLK)],
        ),
        out_shape=partial_shapes(count, planes - base),
        compiler_params=PARAMS,
        cost_estimate=SMALL,
        name="ctx_attend",
    )(info, q, *sources)


def mem_call(info, q, stores, own_lse, ctx_lse, first, count, chunk_first, planes, masked):
    keys = WITHIN * CAP * MROWS
    column = place_of(first, CHUNKS)[1]
    sspec = pl.BlockSpec((stores[0].shape[0], 2 * HD), lambda h, j, info: (0, column + h))
    return pl.pallas_call(
        functools.partial(mem_kernel, masked),
        grid_spec=pltpu.PrefetchScalarGridSpec(
            num_scalar_prefetch=1,
            grid=(count, planes),
            in_specs=[query_spec(first)]
            + [sspec] * WITHIN
            + [
                pl.BlockSpec((1, 1, 8, QBLK), lambda h, j, info: (first + h, 0, 0, 0)),
                pl.BlockSpec((1, 1, 8, QBLK), lambda h, j, info: (first - chunk_first + h, jnp.maximum(j - 1, 0), 0, 0)),
            ],
            out_specs=[per_head(QBLK, QW), per_head(8, QBLK)],
            scratch_shapes=[pltpu.VMEM((keys, HD), jnp.bfloat16), pltpu.VMEM((keys, HD), jnp.bfloat16)],
        ),
        out_shape=partial_shapes(count, planes),
        compiler_params=PARAMS,
        cost_estimate=SMALL,
        name="mem_attend",
    )(info, q, *stores, own_lse, ctx_lse)


def scale_call(info, um, own, uc, gate_rows, lses, first, chunk_first, scattered):
    heads, planes = um.shape[:2]
    part = pl.BlockSpec((heads, 1, QBLK, QW), lambda j, info: (0, j, 0, 0))
    own_part = pl.BlockSpec((heads, 1, QBLK, QW), lambda j, info: (first // heads, 0, 0, 0))
    nth = (first - chunk_first) // heads
    rest = pl.BlockSpec((heads, 1, QBLK, QW), lambda j, info: (nth, jnp.maximum(j - 1, 0), 0, 0))
    if scattered:
        out_specs = [pl.BlockSpec((1, heads, QBLK, QW), lambda j, info: (jnp.bitwise_xor(info[0, 0], j), 0, 0, 0))]
        shapes = [(planes, heads, QBLK, QW)]
    else:
        shapes = [(heads, QBLK, QW)] * planes
        out_specs = [whole(shape) for shape in shapes]
    return pl.pallas_call(
        functools.partial(scale_kernel, planes, heads, scattered),
        grid_spec=pltpu.PrefetchScalarGridSpec(
            num_scalar_prefetch=1,
            grid=(planes,),
            in_specs=[part, own_part, rest, whole((heads, 8, 1))] + [whole((heads, planes, 8, QBLK))] * planes,
            out_specs=out_specs,
        ),
        out_shape=[jax.ShapeDtypeStruct(shape, jnp.bfloat16) for shape in shapes],
        compiler_params=PARAMS,
        cost_estimate=SMALL,
        name="scale_mix",
    )(info, um, own, uc, gate_rows, *lses)


def route_kernel(planes, local_count, ids_ref, slot_ref, place_ref, out_ref):
    entries = slot_ref.shape[0]
    plane, within = place_ref[0], place_ref[1]
    before = lax.broadcasted_iota(jnp.int32, (TOPM, TOPM), 0) <= lax.broadcasted_iota(jnp.int32, (TOPM, TOPM), 1)
    before = before.astype(jnp.float32)
    source = lax.broadcasted_iota(jnp.int32, (8, TOPM), 0)
    holder = plane * WITHIN + jnp.bitwise_xor(within, source)
    lane = lax.broadcasted_iota(jnp.int32, (1, HD), 1)
    for k in range(planes):
        halves = ids_ref[jnp.bitwise_xor(plane, k), :8, : 2 * TOPM].astype(jnp.float32)[:1].astype(jnp.int32)
        ids = halves[:, :TOPM] * 256 + halves[:, TOPM:]
        hits = lax.broadcasted_iota(jnp.int32, (entries, TOPM), 0) == ids
        slots = jnp.sum(jnp.where(hits, slot_ref[...], 0), axis=0, keepdims=True)
        held = (slots // local_count == holder) & (source < WITHIN)
        rank = jnp.dot(held.astype(jnp.float32), before, preferred_element_type=jnp.float32)
        local = slots % local_count + 1
        row = jnp.zeros((1, HD), jnp.int32)
        for r in range(CAP):
            found = jnp.sum(jnp.where(held & (rank == r + 1), local, 0), axis=1, keepdims=True) - 1
            for s in range(WITHIN):
                row = jnp.where(lane == s * CAP + r, found[s : s + 1], row)
        out_ref[k : k + 1, :] = row[:, :8]


def route_call(place, gathered, block_slot, local_count):
    planes = gathered.shape[0]
    return pl.pallas_call(
        functools.partial(route_kernel, planes, local_count),
        grid=(1,),
        in_specs=[
            pl.BlockSpec((planes, ID_ROWS, HD), lambda i: (0, QBLK // ID_ROWS, 0)),
            whole((block_slot.shape[0], 1)),
            pl.BlockSpec(memory_space=pltpu.SMEM),
        ],
        out_specs=whole((planes, 8)),
        out_shape=jax.ShapeDtypeStruct((planes, 8), jnp.int32),
        compiler_params=PARAMS,
        cost_estimate=SMALL,
        name="route_blocks",
    )(gathered, block_slot[:, None], place)


def pack_kernel(stores, chunks, first, q, k, v, ids, *outs):
    for n, heads in enumerate(stores):
        for i, head in enumerate(heads):
            cols = slice(head * HD, (head + 1) * HD)
            outs[n][:, 2 * i * HD : (2 * i + 1) * HD] = k[:, cols]
            outs[n][:, (2 * i + 1) * HD : (2 * i + 2) * HD] = v[:, cols]

    @pl.when(pl.program_id(0) == 0)
    def _():
        for n, heads in enumerate(chunks):
            out = outs[len(stores) + n]
            out[:QBLK, :] = q[:, heads[0] * QW : (heads[-1] + 1) * QW]
            if first and n == 0:
                halves = jnp.concatenate([ids[...] // 256, ids[...] % 256], axis=1).astype(jnp.float32)
                halves = jnp.concatenate([halves, jnp.zeros((1, out.shape[1] - 2 * TOPM), jnp.float32)], axis=1)
                out[QBLK:, :] = jnp.broadcast_to(halves, (ID_ROWS, out.shape[1])).astype(jnp.bfloat16)


def pack_call(stores, chunks, first, q, k, v, ids):
    rows, steps = k.shape[0], 4
    part = rows // steps
    shapes = [(rows, 2 * len(heads) * HD) for heads in stores]
    specs = [pl.BlockSpec((part, shape[1]), lambda i: (i, 0)) for shape in shapes]
    shapes += [(QBLK + ID_ROWS * (first and n == 0), len(heads) * QW) for n, heads in enumerate(chunks)]
    specs += [whole(shape) for shape in shapes[len(stores) :]]
    width = (stores[-1][-1] + 1) * HD
    q_width = (chunks[-1][-1] + 1) * QW if chunks else QW
    return pl.pallas_call(
        functools.partial(pack_kernel, stores, chunks, first),
        grid=(steps,),
        in_specs=[whole((QBLK, q_width))]
        + [pl.BlockSpec((part, width), lambda i: (i, 0))] * 2
        + [whole(ids.shape)],
        out_specs=specs,
        out_shape=[jax.ShapeDtypeStruct(shape, jnp.bfloat16) for shape in shapes],
        compiler_params=PACK_PARAMS,
        cost_estimate=SMALL,
        name="pack_heads",
    )(q, k, v, ids)


class Order:
    def __init__(self):
        self.last = ()

    def before(self, *arrays):
        if not self.last:
            return arrays
        return lax.optimization_barrier((*arrays, *self.last))[: len(arrays)]

    def done(self, *arrays):
        self.last = arrays


def on_device(
    queries, ctx_keys, ctx_values, store_keys, store_values, block_ids, block_slot, gate_logit
):
    devices = lax.axis_size("seq")
    planes = devices // WITHIN
    me = lax.axis_index("seq")
    plane, within = me // WITHIN, me % WITHIN
    local_count = store_keys.shape[0]
    masked = devices * CAP != TOPM

    def xor(x, bits):
        return lax.ppermute(x, "seq", [(i, i ^ bits) for i in range(devices)])

    def all_planes(x):
        return [x] + [xor(x, k * WITHIN) for k in range(1, planes)]

    columns = [[p * WITHIN + w for p in range(planes)] for w in range(WITHIN)]
    keys = store_keys.reshape(local_count * MROWS, KVH * HD)
    values = store_values.reshape(local_count * MROWS, KVH * HD)
    order = Order()

    raw = (queries, keys, values, block_ids)
    ctx_far = [xor(ctx_keys, 2), xor(ctx_values, 2)]
    ctx_near = [xor(ctx_keys, 1), xor(ctx_values, 1)]
    own_first, q_first = pack_call(CHUNKS[:1], CHUNKS[:1], True, *raw)
    order.done(q_first)
    own_second, q_second = pack_call(CHUNKS[1:], CHUNKS[1:], False, *order.before(*raw))
    order.done(q_second, *ctx_far)
    own = [own_first, own_second]
    far = [xor(part, 2) for part in order.before(*own)]
    ctx_diag = [xor(part, 1) for part in ctx_far]
    near = [xor(part, 1) for part in own]
    diag = [None, None]

    gate = 1.0 / (1.0 + jnp.exp(-gate_logit))
    gate_rows = jnp.concatenate([gate.reshape(KVH, G), 1.0 - gate.reshape(KVH, G)], axis=1)[:, :, None]
    spread = [lax.all_gather(part, "seq", axis=0, axis_index_groups=columns) for part in (q_first, q_second)]

    place = jnp.stack([plane, within] + [plane] * 6).astype(jnp.int32)
    route = route_call(place, spread[0], block_slot, local_count)
    place = place[None]
    info = jnp.concatenate([place, route])
    sources = [x for kind in zip((ctx_keys, ctx_values), ctx_near, ctx_far, ctx_diag, strict=True) for x in kind]

    def fetch_step(n):
        (far[n],) = order.before(far[n])
        order.done(far[n])
        diag[n] = xor(far[n], 1)

    def ctx_step(q, first, count, slots):
        args = order.before(place, q, *sources)
        uc, lse = ctx_call(args[0], args[1], args[2:], first, count, slots)
        order.done(lse)
        return uc, lse

    def mem_step(first, count, ctx_lse):
        n = place_of(first, CHUNKS)[0]
        args = order.before(info, spread[n], own[n], near[n], far[n], diag[n], own_lse, ctx_lse)
        um, lse = mem_call(*args[:2], args[2:6], *args[6:], first, count, CHUNKS[n][0], planes, masked)
        order.done(lse)
        return um, all_planes(lse)

    def scale_step(first, um, uc, lses, scattered):
        n = place_of(first, CHUNKS)[0]
        um, uc, *lses = order.before(um, uc, *lses)
        gates = gate_rows[first : first + um.shape[0]]
        parts = scale_call(place, um, own_uc, uc, gates, lses, first, CHUNKS[n][0], scattered)
        order.done(parts[0])
        if scattered:
            return [lax.psum_scatter(parts[0], "seq", scatter_dimension=0, axis_index_groups=columns)]
        return [parts[0]] + [xor(parts[k], k * WITHIN) for k in range(1, planes)]

    def total(parts):
        return sum(part.astype(jnp.float32) for part in parts).astype(jnp.bfloat16)

    own_uc, own_lse = ctx_step(queries, 0, KVH, 1)
    uc01, ctx_lse01 = ctx_step(spread[0], 0, 2, planes)
    fetch_step(0)
    um01, lses01 = mem_step(0, 2, ctx_lse01)
    coming = [scale_step(0, um01, uc01, lses01, True)]
    uc23, ctx_lse23 = ctx_step(spread[1], 2, 2, planes)
    fetch_step(1)
    um2, lses2 = mem_step(2, 1, ctx_lse23)
    um3, lses3 = mem_step(3, 1, ctx_lse23)
    coming.append(scale_step(2, um2, uc23, lses2, True))
    coming.append(scale_step(3, um3, uc23, lses3, False))
    return jnp.concatenate([part for parts in coming for part in total(parts)], axis=1)


def solution(mesh):
    placed = (
        P(("groups", "seq"), None),
        P(("groups", "seq"), None),
        P(("groups", "seq"), None),
        P(("groups", "seq"), None, None),
        P(("groups", "seq"), None, None),
        P(("groups", "seq"), None),
        P("groups"),
        P(),
    )
    return jax.shard_map(
        on_device, mesh=mesh, in_specs=placed, out_specs=P(("groups", "seq"), None), check_vma=False
    )
```

```python
import functools

import jax
import jax.numpy as jnp
from jax import lax
from jax.experimental import pallas as pl
from jax.experimental.pallas import tpu as pltpu
from jax.sharding import PartitionSpec as P

H = 16
KVH = 4
HD = 128
QBLK = 256
MROWS = 128
TOPM = 32
CAP = 2
G = H // KVH
WITHIN = 4
LOG2E = 1.4426950408889634
SCALE = HD**-0.5 * LOG2E
MASKED = -1e30
QW = G * HD
CHUNKS = ((0, 1), (2, 3))
GROUPS = (((0, 1), "scatter"), ((2,), "direct"), ((3,), "direct"))


def scores_of(q, k):
    return lax.dot_general(q, k, (((1,), (1,)), ((), ())), preferred_element_type=jnp.float32)


def attend_heads(q, k, v, allowed, out_ref):
    keys = k.shape[0]
    vx = jnp.concatenate([v, jnp.ones((keys, HD), jnp.bfloat16)], axis=1)
    lane = lax.broadcasted_iota(jnp.int32, (QBLK, HD), 1)
    rows = jnp.zeros((QBLK, HD), jnp.float32)
    ahead = scores_of(q[:, :HD], k)
    for g in range(G):
        s = ahead
        if g + 1 < G:
            ahead = scores_of(q[:, (g + 1) * HD : (g + 2) * HD], k)
        if allowed is not None:
            s = jnp.where(allowed, s, MASKED)
        m = jnp.max(s, axis=1, keepdims=True)
        p = jnp.exp2((s - m) * SCALE).astype(jnp.bfloat16)
        o = jnp.dot(p, vx, preferred_element_type=jnp.float32)
        total = o[:, HD:]
        out_ref[0, :, g * HD : (g + 1) * HD] = (o[:, :HD] / total).astype(jnp.bfloat16)
        rows = jnp.where(lane == g, m * SCALE + jnp.log2(total), rows)
    return rows.T[:8]


def ctx_kernel(slot_base, info, q_ref, k0, k1, k2, k3, v0, v1, v2, v3, out_ref, lse_ref):
    slot = pl.program_id(1) + slot_base
    plane, within = info[0, 0], info[0, 1]
    target = jnp.bitwise_xor(plane, slot)

    def run(allowed):
        k = jnp.concatenate([k0[...], k1[...], k2[...], k3[...]], axis=0)
        v = jnp.concatenate([v0[...], v1[...], v2[...], v3[...]], axis=0)
        lse_ref[0, 0] = attend_heads(q_ref[0] if slot_base else q_ref[...], k, v, allowed, out_ref.at[0])

    if slot_base == 0:
        keys = WITHIN * QBLK
        col = lax.broadcasted_iota(jnp.int32, (QBLK, keys), 1)
        row = lax.broadcasted_iota(jnp.int32, (QBLK, keys), 0)
        key_pos = jnp.bitwise_xor(col // QBLK, within) * QBLK + col % QBLK
        run(key_pos <= within * QBLK + row)
        return

    @pl.when(target > plane)
    def _():
        run(None)

    @pl.when(target < plane)
    def _():
        out_ref[...] = jnp.zeros_like(out_ref)
        lse_ref[...] = jnp.full_like(lse_ref, MASKED)


def mem_kernel(masked, info, q_ref, s0, s1, s2, s3, own_lse_ref, ctx_lse_ref, out_ref, lse_ref, kbuf, vbuf):
    slot = pl.program_id(1)
    stores = (s0, s1, s2, s3)
    allowed = None
    keys = WITHIN * CAP * MROWS
    if masked:
        col = lax.broadcasted_iota(jnp.int32, (QBLK, keys), 1) // MROWS
        allowed = jnp.zeros((QBLK, keys), jnp.bool_)
    for n in range(WITHIN * CAP):
        entry = info[1 + slot, n]
        start = pl.multiple_of(jnp.maximum(entry, 0) * MROWS, MROWS)
        rows, to = pl.ds(start, MROWS), slice(n * MROWS, (n + 1) * MROWS)
        kbuf[to, :] = stores[n // CAP][rows, :HD]
        vbuf[to, :] = stores[n // CAP][rows, HD:]
        if masked:
            allowed = allowed | ((col == n) & (entry >= 0))
    lse_ref[0, 0] = attend_heads(q_ref[0], kbuf[...], vbuf[...], allowed, out_ref.at[0])
    lse_ref[0, 0, G:] = jnp.where(slot == 0, own_lse_ref[0, 0, :G], ctx_lse_ref[0, 0, :G])


def scale_kernel(planes, heads, scattered, info, um_ref, own_ref, uc_ref, gate_ref, *refs):
    lse_refs, out_refs = refs[:planes], refs[planes:]
    slot = pl.program_id(0)
    row = lax.broadcasted_iota(jnp.int32, (16, 2 * QW), 0) % 8
    spread = (row == lax.broadcasted_iota(jnp.int32, (16, 2 * QW), 1) // HD).astype(jnp.bfloat16)
    for h in range(heads):
        parts = [lse_refs[k][h, jnp.bitwise_xor(slot, k)] for k in range(planes)]
        top = functools.reduce(jnp.maximum, parts)
        total = functools.reduce(jnp.add, [jnp.exp2(p - top) for p in parts])
        weight = jnp.exp2(parts[0] - top) / total * gate_ref[h]
        high = weight.astype(jnp.bfloat16)
        low = (weight - high.astype(jnp.float32)).astype(jnp.bfloat16)
        wide = lax.dot_general(
            jnp.concatenate([high, low], axis=0), spread, (((0,), (0,)), ((), ())), preferred_element_type=jnp.float32
        )
        for g in range(G):
            cols = slice(g * HD, (g + 1) * HD)
            term = wide[:, cols] * um_ref[h, 0, :, cols].astype(jnp.float32)
            ctx = jnp.where(slot == 0, own_ref[h, 0, :, cols], uc_ref[h, 0, :, cols])
            term += wide[:, QW + g * HD : QW + (g + 1) * HD] * ctx.astype(jnp.float32)
            term = term.astype(jnp.bfloat16)
            if scattered:
                out_refs[0][0, h, :, cols] = term
                continue
            for i, ref in enumerate(out_refs):

                @pl.when(slot == i)
                def _(ref=ref):
                    ref[h, :, cols] = term


PARAMS = pltpu.CompilerParams(vmem_limit_bytes=56 * 1024 * 1024)
PACK_PARAMS = pltpu.CompilerParams(vmem_limit_bytes=60 * 1024 * 1024)
SMALL = pl.CostEstimate(flops=1000, bytes_accessed=1000, transcendentals=0)


def place_of(head, chunks):
    return next((n, heads.index(head)) for n, heads in enumerate(chunks) if head in heads)


def whole(shape):
    return pl.BlockSpec(shape, lambda *_: (0,) * len(shape))


def query_spec(first):
    column = place_of(first, CHUNKS)[1]
    return pl.BlockSpec((1, QBLK, QW), lambda h, j, info: (jnp.bitwise_xor(info[0, 0], j), 0, column + h))


def per_head(rows, cols):
    return pl.BlockSpec((1, 1, rows, cols), lambda h, j, info: (h, j, 0, 0))


def partial_shapes(count, planes):
    return [
        jax.ShapeDtypeStruct((count, planes, QBLK, QW), jnp.bfloat16),
        jax.ShapeDtypeStruct((count, planes, 8, QBLK), jnp.float32),
    ]


def ctx_call(info, q, sources, first, count, planes):
    base = min(planes - 1, 1)
    kspec = pl.BlockSpec((QBLK, HD), lambda h, j, info: (0, first + h))
    if base:
        column = place_of(first, CHUNKS)[1]
        qspec = pl.BlockSpec((1, QBLK, QW), lambda h, j, info: (jnp.bitwise_xor(info[0, 0], j + 1), 0, column + h))
    else:
        qspec = pl.BlockSpec((QBLK, QW), lambda h, j, info: (0, first + h))
    return pl.pallas_call(
        functools.partial(ctx_kernel, base),
        grid_spec=pltpu.PrefetchScalarGridSpec(
            num_scalar_prefetch=1,
            grid=(count, planes - base),
            in_specs=[qspec] + [kspec] * (2 * WITHIN),
            out_specs=[per_head(QBLK, QW), per_head(8, QBLK)],
        ),
        out_shape=partial_shapes(count, planes - base),
        compiler_params=PARAMS,
        cost_estimate=SMALL,
        name="ctx_attend",
    )(info, q, *sources)


def mem_call(info, q, stores, own_lse, ctx_lse, first, count, chunk_first, planes, masked):
    keys = WITHIN * CAP * MROWS
    column = place_of(first, CHUNKS)[1]
    sspec = pl.BlockSpec((stores[0].shape[0], 2 * HD), lambda h, j, info: (0, column + h))
    return pl.pallas_call(
        functools.partial(mem_kernel, masked),
        grid_spec=pltpu.PrefetchScalarGridSpec(
            num_scalar_prefetch=1,
            grid=(count, planes),
            in_specs=[query_spec(first)]
            + [sspec] * WITHIN
            + [
                pl.BlockSpec((1, 1, 8, QBLK), lambda h, j, info: (first + h, 0, 0, 0)),
                pl.BlockSpec((1, 1, 8, QBLK), lambda h, j, info: (first - chunk_first + h, jnp.maximum(j - 1, 0), 0, 0)),
            ],
            out_specs=[per_head(QBLK, QW), per_head(8, QBLK)],
            scratch_shapes=[pltpu.VMEM((keys, HD), jnp.bfloat16), pltpu.VMEM((keys, HD), jnp.bfloat16)],
        ),
        out_shape=partial_shapes(count, planes),
        compiler_params=PARAMS,
        cost_estimate=SMALL,
        name="mem_attend",
    )(info, q, *stores, own_lse, ctx_lse)


def scale_call(info, um, own, uc, gate_rows, lses, first, chunk_first, scattered):
    heads, planes = um.shape[:2]
    part = pl.BlockSpec((heads, 1, QBLK, QW), lambda j, info: (0, j, 0, 0))
    own_part = pl.BlockSpec((heads, 1, QBLK, QW), lambda j, info: (first // heads, 0, 0, 0))
    nth = (first - chunk_first) // heads
    rest = pl.BlockSpec((heads, 1, QBLK, QW), lambda j, info: (nth, jnp.maximum(j - 1, 0), 0, 0))
    if scattered:
        out_specs = [pl.BlockSpec((1, heads, QBLK, QW), lambda j, info: (jnp.bitwise_xor(info[0, 0], j), 0, 0, 0))]
        shapes = [(planes, heads, QBLK, QW)]
    else:
        shapes = [(heads, QBLK, QW)] * planes
        out_specs = [whole(shape) for shape in shapes]
    return pl.pallas_call(
        functools.partial(scale_kernel, planes, heads, scattered),
        grid_spec=pltpu.PrefetchScalarGridSpec(
            num_scalar_prefetch=1,
            grid=(planes,),
            in_specs=[part, own_part, rest, whole((heads, 8, 1))] + [whole((heads, planes, 8, QBLK))] * planes,
            out_specs=out_specs,
        ),
        out_shape=[jax.ShapeDtypeStruct(shape, jnp.bfloat16) for shape in shapes],
        compiler_params=PARAMS,
        cost_estimate=SMALL,
        name="scale_mix",
    )(info, um, own, uc, gate_rows, *lses)


def route_kernel(planes, local_count, *refs):
    ids_refs, (slot_ref, place_ref, out_ref) = refs[:planes], refs[planes:]
    entries = slot_ref.shape[0]
    plane, within = place_ref[0], place_ref[1]
    before = lax.broadcasted_iota(jnp.int32, (TOPM, TOPM), 0) <= lax.broadcasted_iota(jnp.int32, (TOPM, TOPM), 1)
    before = before.astype(jnp.float32)
    source = lax.broadcasted_iota(jnp.int32, (8, TOPM), 0)
    holder = plane * WITHIN + jnp.bitwise_xor(within, source)
    lane = lax.broadcasted_iota(jnp.int32, (1, HD), 1)
    for k in range(planes):
        hits = lax.broadcasted_iota(jnp.int32, (entries, TOPM), 0) == ids_refs[k][...]
        slots = jnp.sum(jnp.where(hits, slot_ref[...], 0), axis=0, keepdims=True)
        held = (slots // local_count == holder) & (source < WITHIN)
        rank = jnp.dot(held.astype(jnp.float32), before, preferred_element_type=jnp.float32)
        local = slots % local_count + 1
        row = jnp.zeros((1, HD), jnp.int32)
        for r in range(CAP):
            found = jnp.sum(jnp.where(held & (rank == r + 1), local, 0), axis=1, keepdims=True) - 1
            for s in range(WITHIN):
                row = jnp.where(lane == s * CAP + r, found[s : s + 1], row)
        out_ref[k : k + 1, :] = row[:, :8]


def route_call(place, ids, block_slot, local_count):
    planes = len(ids)
    return pl.pallas_call(
        functools.partial(route_kernel, planes, local_count),
        grid=(1,),
        in_specs=[whole((1, TOPM))] * planes
        + [whole((block_slot.shape[0], 1)), pl.BlockSpec(memory_space=pltpu.SMEM)],
        out_specs=whole((planes, 8)),
        out_shape=jax.ShapeDtypeStruct((planes, 8), jnp.int32),
        compiler_params=PARAMS,
        cost_estimate=SMALL,
        name="route_blocks",
    )(*ids, block_slot[:, None], place)


def pack_queries_kernel(q, *outs):
    for out, heads in zip(outs, CHUNKS, strict=True):
        out[...] = q[:, heads[0] * QW : (heads[-1] + 1) * QW]


def pack_queries(q):
    shapes = [(QBLK, len(heads) * QW) for heads in CHUNKS]
    return pl.pallas_call(
        pack_queries_kernel,
        grid=(1,),
        in_specs=[whole(q.shape)],
        out_specs=[whole(shape) for shape in shapes],
        out_shape=[jax.ShapeDtypeStruct(shape, jnp.bfloat16) for shape in shapes],
        compiler_params=PACK_PARAMS,
        cost_estimate=SMALL,
        name="pack_queries",
    )(q)


def pack_stores_kernel(k, v, out):
    for i in range(k.shape[1] // HD):
        cols = slice(i * HD, (i + 1) * HD)
        out[:, 2 * i * HD : (2 * i + 1) * HD] = k[:, cols]
        out[:, (2 * i + 1) * HD : (2 * i + 2) * HD] = v[:, cols]


def pack_stores(k, v, n):
    rows, steps = k.shape[0], 4
    part, width = rows // steps, len(CHUNKS[n]) * HD
    return pl.pallas_call(
        pack_stores_kernel,
        grid=(steps,),
        in_specs=[pl.BlockSpec((part, width), lambda i: (i, n))] * 2,
        out_specs=pl.BlockSpec((part, 2 * width), lambda i: (i, 0)),
        out_shape=jax.ShapeDtypeStruct((rows, 2 * width), jnp.bfloat16),
        compiler_params=PACK_PARAMS,
        cost_estimate=SMALL,
        name="pack_stores",
    )(k, v)


def finish_kernel(counts, *refs):
    *parts, out_ref = refs
    head = 0
    for count, heads in counts:
        group, parts = parts[:count], parts[count:]
        for h in range(heads):
            total = group[0][h]
            if count > 1:
                total = sum(part[h].astype(jnp.float32) for part in group).astype(jnp.bfloat16)
            out_ref[:, (head + h) * QW : (head + h + 1) * QW] = total
        head += heads


def finish_call(groups):
    flat = [part for parts in groups for part in parts]
    return pl.pallas_call(
        functools.partial(finish_kernel, [(len(parts), parts[0].shape[0]) for parts in groups]),
        grid=(1,),
        in_specs=[whole(part.shape) for part in flat],
        out_specs=whole((QBLK, KVH * QW)),
        out_shape=jax.ShapeDtypeStruct((QBLK, KVH * QW), jnp.bfloat16),
        compiler_params=PARAMS,
        cost_estimate=SMALL,
        name="finish_heads",
    )(*flat)


class Order:
    def __init__(self):
        self.last = ()

    def before(self, *arrays):
        if not self.last:
            return arrays
        return lax.optimization_barrier((*arrays, *self.last))[: len(arrays)]

    def done(self, *arrays):
        self.last = arrays


def on_device(
    queries, ctx_keys, ctx_values, store_keys, store_values, block_ids, block_slot, gate_logit
):
    devices = lax.axis_size("seq")
    planes = devices // WITHIN
    me = lax.axis_index("seq")
    plane, within = me // WITHIN, me % WITHIN
    local_count = store_keys.shape[0]
    masked = devices * CAP != TOPM

    def xor(x, bits):
        return lax.ppermute(x, "seq", [(i, i ^ bits) for i in range(devices)])

    def all_planes(x):
        return [x] + [xor(x, k * WITHIN) for k in range(1, planes)]

    columns = [[p * WITHIN + w for p in range(planes)] for w in range(WITHIN)]
    keys = store_keys.reshape(local_count * MROWS, KVH * HD)
    values = store_values.reshape(local_count * MROWS, KVH * HD)
    order = Order()

    ctx_far = [xor(ctx_keys, 2), xor(ctx_values, 2)]
    ctx_near = [xor(ctx_keys, 1), xor(ctx_values, 1)]
    ids = all_planes(block_ids)
    q_first, q_second = pack_queries(queries)
    order.done(q_first)
    own = [pack_stores(*order.before(keys, values), 0)]
    order.done(own[0], *ctx_far)
    far = [xor(order.before(own[0])[0], 2)]
    own.append(pack_stores(*order.before(keys, values), 1))
    order.done(own[1])
    far.append(xor(own[1], 2))
    ctx_diag = [xor(part, 1) for part in ctx_far]
    near = [xor(part, 1) for part in own]
    diag = [None, None]

    gate = 1.0 / (1.0 + jnp.exp(-gate_logit))
    gate_rows = jnp.concatenate([gate.reshape(KVH, G), 1.0 - gate.reshape(KVH, G)], axis=1)[:, :, None]
    spread = [lax.all_gather(part, "seq", axis=0, axis_index_groups=columns) for part in (q_first, q_second)]

    place = jnp.stack([plane, within] + [plane] * 6).astype(jnp.int32)
    route = route_call(place, order.before(*ids), block_slot, local_count)
    order.done(route)
    place = place[None]
    info = jnp.concatenate([place, route])
    sources = [x for kind in zip((ctx_keys, ctx_values), ctx_near, ctx_far, ctx_diag, strict=True) for x in kind]

    def fetch_step(n):
        (far[n],) = order.before(far[n])
        order.done(far[n])
        diag[n] = xor(far[n], 1)

    def ctx_step(q, first, count, slots):
        args = order.before(place, q, *sources)
        uc, lse = ctx_call(args[0], args[1], args[2:], first, count, slots)
        order.done(lse)
        return uc, lse

    def mem_step(first, count, ctx_lse):
        n = place_of(first, CHUNKS)[0]
        args = order.before(info, spread[n], own[n], near[n], far[n], diag[n], own_lse, ctx_lse)
        um, lse = mem_call(*args[:2], args[2:6], *args[6:], first, count, CHUNKS[n][0] if count > 1 else first, planes, masked)
        order.done(lse)
        return um, all_planes(lse)

    def scale_step(first, um, uc, lses, scattered):
        n = place_of(first, CHUNKS)[0]
        um, uc, *lses = order.before(um, uc, *lses)
        gates = gate_rows[first : first + um.shape[0]]
        parts = scale_call(place, um, own_uc, uc, gates, lses, first, first, scattered)
        order.done(parts[0])
        if scattered:
            return [lax.psum_scatter(parts[0], "seq", scatter_dimension=0, axis_index_groups=columns)]
        return [parts[0]] + [xor(parts[k], k * WITHIN) for k in range(1, planes)]

    own_uc, own_lse = ctx_step(queries, 0, KVH, 1)
    uc01, ctx_lse01 = ctx_step(spread[0], 0, 2, planes)
    fetch_step(0)
    um01, lses01 = mem_step(0, 2, ctx_lse01)
    coming = [scale_step(0, um01, uc01, lses01, True)]
    uc2, ctx_lse2 = ctx_step(spread[1], 2, 1, planes)
    fetch_step(1)
    uc3, ctx_lse3 = ctx_step(spread[1], 3, 1, planes)
    um2, lses2 = mem_step(2, 1, ctx_lse2)
    um3, lses3 = mem_step(3, 1, ctx_lse3)
    coming.append(scale_step(2, um2, uc2, lses2, True))
    coming.append(scale_step(3, um3, uc3, lses3, False))
    return finish_call(coming)


def solution(mesh):
    placed = (
        P(("groups", "seq"), None),
        P(("groups", "seq"), None),
        P(("groups", "seq"), None),
        P(("groups", "seq"), None, None),
        P(("groups", "seq"), None, None),
        P(("groups", "seq"), None),
        P("groups"),
        P(),
    )
    return jax.shard_map(
        on_device, mesh=mesh, in_specs=placed, out_specs=P(("groups", "seq"), None), check_vma=False
    )
```

```python
import functools

import jax
import jax.numpy as jnp
from jax import lax
from jax.experimental import pallas as pl
from jax.experimental.pallas import tpu as pltpu
from jax.sharding import PartitionSpec as P

H = 16
KVH = 4
HD = 128
QBLK = 256
MROWS = 128
TOPM = 32
CAP = 2
G = H // KVH
WITHIN = 4
LOG2E = 1.4426950408889634
SCALE = HD**-0.5 * LOG2E
MASKED = -1e30
QW = G * HD
CHUNKS = ((0, 1), (2, 3))
GROUPS = (((0, 1), "scatter"), ((2,), "direct"), ((3,), "direct"))


def scores_of(q, k):
    return lax.dot_general(q, k, (((1,), (1,)), ((), ())), preferred_element_type=jnp.float32)


def attend_heads(q, k, v, allowed, out_ref):
    keys = k.shape[0]
    vx = jnp.concatenate([v, jnp.ones((keys, HD), jnp.bfloat16)], axis=1)
    lane = lax.broadcasted_iota(jnp.int32, (QBLK, HD), 1)
    rows = jnp.zeros((QBLK, HD), jnp.float32)
    ahead = scores_of(q[:, :HD], k)
    for g in range(G):
        s = ahead
        if g + 1 < G:
            ahead = scores_of(q[:, (g + 1) * HD : (g + 2) * HD], k)
        if allowed is not None:
            s = jnp.where(allowed, s, MASKED)
        m = jnp.max(s, axis=1, keepdims=True)
        p = jnp.exp2((s - m) * SCALE).astype(jnp.bfloat16)
        o = jnp.dot(p, vx, preferred_element_type=jnp.float32)
        total = o[:, HD:]
        out_ref[0, :, g * HD : (g + 1) * HD] = (o[:, :HD] / total).astype(jnp.bfloat16)
        rows = jnp.where(lane == g, m * SCALE + jnp.log2(total), rows)
    return rows.T[:8]


def ctx_kernel(slot_base, info, q_ref, k0, k1, k2, k3, v0, v1, v2, v3, out_ref, lse_ref):
    slot = pl.program_id(1) + slot_base
    plane, within = info[0, 0], info[0, 1]
    target = jnp.bitwise_xor(plane, slot)

    def run(allowed):
        k = jnp.concatenate([k0[...], k1[...], k2[...], k3[...]], axis=0)
        v = jnp.concatenate([v0[...], v1[...], v2[...], v3[...]], axis=0)
        lse_ref[0, 0] = attend_heads(q_ref[0] if slot_base else q_ref[...], k, v, allowed, out_ref.at[0])

    if slot_base == 0:
        keys = WITHIN * QBLK
        col = lax.broadcasted_iota(jnp.int32, (QBLK, keys), 1)
        row = lax.broadcasted_iota(jnp.int32, (QBLK, keys), 0)
        key_pos = jnp.bitwise_xor(col // QBLK, within) * QBLK + col % QBLK
        run(key_pos <= within * QBLK + row)
        return

    @pl.when(target > plane)
    def _():
        run(None)

    @pl.when(target < plane)
    def _():
        out_ref[...] = jnp.zeros_like(out_ref)
        lse_ref[...] = jnp.full_like(lse_ref, MASKED)


def mem_kernel(masked, info, q_ref, s0, s1, s2, s3, own_lse_ref, ctx_lse_ref, out_ref, lse_ref, kbuf, vbuf):
    slot = pl.program_id(1)
    stores = (s0, s1, s2, s3)
    allowed = None
    keys = WITHIN * CAP * MROWS
    if masked:
        col = lax.broadcasted_iota(jnp.int32, (QBLK, keys), 1) // MROWS
        allowed = jnp.zeros((QBLK, keys), jnp.bool_)
    for n in range(WITHIN * CAP):
        entry = info[1 + slot, n]
        start = pl.multiple_of(jnp.maximum(entry, 0) * MROWS, MROWS)
        rows, to = pl.ds(start, MROWS), slice(n * MROWS, (n + 1) * MROWS)
        kbuf[to, :] = stores[n // CAP][rows, :HD]
        vbuf[to, :] = stores[n // CAP][rows, HD:]
        if masked:
            allowed = allowed | ((col == n) & (entry >= 0))
    lse_ref[0, 0] = attend_heads(q_ref[0], kbuf[...], vbuf[...], allowed, out_ref.at[0])
    lse_ref[0, 0, G:] = jnp.where(slot == 0, own_lse_ref[0, 0, :G], ctx_lse_ref[0, 0, :G])


def scale_kernel(planes, heads, first, scattered, info, um_ref, own_ref, uc_ref, gate_ref, *refs):
    lse_refs, out_refs = refs[:planes], refs[planes:]
    slot = pl.program_id(0)
    part_row = lax.broadcasted_iota(jnp.int32, (8, QBLK), 0)
    row = lax.broadcasted_iota(jnp.int32, (16, 2 * QW), 0) % 8
    spread = (row == lax.broadcasted_iota(jnp.int32, (16, 2 * QW), 1) // HD).astype(jnp.bfloat16)
    for h in range(heads):
        parts = [lse_refs[k][h, jnp.bitwise_xor(slot, k)] for k in range(planes)]
        top = functools.reduce(jnp.maximum, parts)
        total = functools.reduce(jnp.add, [jnp.exp2(p - top) for p in parts])
        weight = jnp.exp2(parts[0] - top) / total
        for g in range(G):
            gate = gate_ref[(first + h) * G + g]
            weight = jnp.where(part_row == g, weight * gate, weight)
            weight = jnp.where(part_row == G + g, weight * (1.0 - gate), weight)
        high = weight.astype(jnp.bfloat16)
        low = (weight - high.astype(jnp.float32)).astype(jnp.bfloat16)
        wide = lax.dot_general(
            jnp.concatenate([high, low], axis=0), spread, (((0,), (0,)), ((), ())), preferred_element_type=jnp.float32
        )
        for g in range(G):
            cols = slice(g * HD, (g + 1) * HD)
            term = wide[:, cols] * um_ref[h, 0, :, cols].astype(jnp.float32)
            ctx = jnp.where(slot == 0, own_ref[h, 0, :, cols], uc_ref[h, 0, :, cols])
            term += wide[:, QW + g * HD : QW + (g + 1) * HD] * ctx.astype(jnp.float32)
            term = term.astype(jnp.bfloat16)
            if scattered:
                out_refs[0][0, h, :, cols] = term
                continue
            for i, ref in enumerate(out_refs):

                @pl.when(slot == i)
                def _(ref=ref):
                    ref[h, :, cols] = term


PARAMS = pltpu.CompilerParams(vmem_limit_bytes=24 * 1024 * 1024)
PACK_PARAMS = pltpu.CompilerParams(vmem_limit_bytes=60 * 1024 * 1024)
SMALL = pl.CostEstimate(flops=1000, bytes_accessed=1000, transcendentals=0)


def place_of(head, chunks):
    return next((n, heads.index(head)) for n, heads in enumerate(chunks) if head in heads)


def whole(shape):
    return pl.BlockSpec(shape, lambda *_: (0,) * len(shape))


def query_spec(first):
    column = place_of(first, CHUNKS)[1]
    return pl.BlockSpec((1, QBLK, QW), lambda h, j, info: (jnp.bitwise_xor(info[0, 0], j), 0, column + h))


def per_head(rows, cols):
    return pl.BlockSpec((1, 1, rows, cols), lambda h, j, info: (h, j, 0, 0))


def partial_shapes(count, planes):
    return [
        jax.ShapeDtypeStruct((count, planes, QBLK, QW), jnp.bfloat16),
        jax.ShapeDtypeStruct((count, planes, 8, QBLK), jnp.float32),
    ]


def ctx_call(info, q, sources, first, count, planes):
    base = min(planes - 1, 1)
    kspec = pl.BlockSpec((QBLK, HD), lambda h, j, info: (0, first + h))
    if base:
        column = place_of(first, CHUNKS)[1]
        qspec = pl.BlockSpec((1, QBLK, QW), lambda h, j, info: (jnp.bitwise_xor(info[0, 0], j + 1), 0, column + h))
    else:
        qspec = pl.BlockSpec((QBLK, QW), lambda h, j, info: (0, first + h))
    return pl.pallas_call(
        functools.partial(ctx_kernel, base),
        grid_spec=pltpu.PrefetchScalarGridSpec(
            num_scalar_prefetch=1,
            grid=(count, planes - base),
            in_specs=[qspec] + [kspec] * (2 * WITHIN),
            out_specs=[per_head(QBLK, QW), per_head(8, QBLK)],
        ),
        out_shape=partial_shapes(count, planes - base),
        compiler_params=PACK_PARAMS,
        cost_estimate=SMALL,
        name="ctx_attend",
    )(info, q, *sources)


def mem_call(info, q, stores, own_lse, ctx_lse, first, count, chunk_first, planes, masked):
    keys = WITHIN * CAP * MROWS
    column = place_of(first, CHUNKS)[1]
    sspec = pl.BlockSpec((stores[0].shape[0], 2 * HD), lambda h, j, info: (0, column + h))
    return pl.pallas_call(
        functools.partial(mem_kernel, masked),
        grid_spec=pltpu.PrefetchScalarGridSpec(
            num_scalar_prefetch=1,
            grid=(count, planes),
            in_specs=[query_spec(first)]
            + [sspec] * WITHIN
            + [
                pl.BlockSpec((1, 1, 8, QBLK), lambda h, j, info: (first + h, 0, 0, 0)),
                pl.BlockSpec((1, 1, 8, QBLK), lambda h, j, info: (first - chunk_first + h, jnp.maximum(j - 1, 0), 0, 0)),
            ],
            out_specs=[per_head(QBLK, QW), per_head(8, QBLK)],
            scratch_shapes=[pltpu.VMEM((keys, HD), jnp.bfloat16), pltpu.VMEM((keys, HD), jnp.bfloat16)],
        ),
        out_shape=partial_shapes(count, planes),
        compiler_params=PARAMS,
        cost_estimate=SMALL,
        name="mem_attend",
    )(info, q, *stores, own_lse, ctx_lse)


def scale_call(info, um, own, uc, gate, lses, first, chunk_first, scattered):
    heads, planes = um.shape[:2]
    part = pl.BlockSpec((heads, 1, QBLK, QW), lambda j, info: (0, j, 0, 0))
    own_part = pl.BlockSpec((heads, 1, QBLK, QW), lambda j, info: (first // heads, 0, 0, 0))
    nth = (first - chunk_first) // heads
    rest = pl.BlockSpec((heads, 1, QBLK, QW), lambda j, info: (nth, jnp.maximum(j - 1, 0), 0, 0))
    if scattered:
        out_specs = [pl.BlockSpec((1, heads, QBLK, QW), lambda j, info: (jnp.bitwise_xor(info[0, 0], j), 0, 0, 0))]
        shapes = [(planes, heads, QBLK, QW)]
    else:
        shapes = [(heads, QBLK, QW)] * planes
        out_specs = [whole(shape) for shape in shapes]
    return pl.pallas_call(
        functools.partial(scale_kernel, planes, heads, first, scattered),
        grid_spec=pltpu.PrefetchScalarGridSpec(
            num_scalar_prefetch=1,
            grid=(planes,),
            in_specs=[part, own_part, rest, pl.BlockSpec(memory_space=pltpu.SMEM)] + [whole((heads, planes, 8, QBLK))] * planes,
            out_specs=out_specs,
        ),
        out_shape=[jax.ShapeDtypeStruct(shape, jnp.bfloat16) for shape in shapes],
        compiler_params=PARAMS,
        cost_estimate=SMALL,
        name="scale_mix",
    )(info, um, own, uc, gate, *lses)


def route_kernel(planes, local_count, *refs):
    ids_refs, (slot_ref, place_ref, out_ref) = refs[:planes], refs[planes:]
    entries = slot_ref.shape[0]
    plane, within = place_ref[0], place_ref[1]
    before = lax.broadcasted_iota(jnp.int32, (TOPM, TOPM), 0) <= lax.broadcasted_iota(jnp.int32, (TOPM, TOPM), 1)
    before = before.astype(jnp.float32)
    source = lax.broadcasted_iota(jnp.int32, (8, TOPM), 0)
    holder = plane * WITHIN + jnp.bitwise_xor(within, source)
    lane = lax.broadcasted_iota(jnp.int32, (1, HD), 1)
    for k in range(planes):
        hits = lax.broadcasted_iota(jnp.int32, (entries, TOPM), 0) == ids_refs[k][...]
        slots = jnp.sum(jnp.where(hits, slot_ref[...], 0), axis=0, keepdims=True)
        held = (slots // local_count == holder) & (source < WITHIN)
        rank = jnp.dot(held.astype(jnp.float32), before, preferred_element_type=jnp.float32)
        local = slots % local_count + 1
        row = jnp.zeros((1, HD), jnp.int32)
        for r in range(CAP):
            found = jnp.sum(jnp.where(held & (rank == r + 1), local, 0), axis=1, keepdims=True) - 1
            for s in range(WITHIN):
                row = jnp.where(lane == s * CAP + r, found[s : s + 1], row)
        out_ref[k : k + 1, :] = row[:, :8]


def route_call(place, ids, block_slot, local_count):
    planes = len(ids)
    return pl.pallas_call(
        functools.partial(route_kernel, planes, local_count),
        grid=(1,),
        in_specs=[whole((1, TOPM))] * planes
        + [whole((block_slot.shape[0], 1)), pl.BlockSpec(memory_space=pltpu.SMEM)],
        out_specs=whole((planes, 8)),
        out_shape=jax.ShapeDtypeStruct((planes, 8), jnp.int32),
        compiler_params=PARAMS,
        cost_estimate=SMALL,
        name="route_blocks",
    )(*ids, block_slot[:, None], place)


def pack_queries_kernel(q, *outs):
    for out, heads in zip(outs, CHUNKS, strict=True):
        out[...] = q[:, heads[0] * QW : (heads[-1] + 1) * QW]


def pack_queries(q):
    shapes = [(QBLK, len(heads) * QW) for heads in CHUNKS]
    return pl.pallas_call(
        pack_queries_kernel,
        grid=(1,),
        in_specs=[whole(q.shape)],
        out_specs=[whole(shape) for shape in shapes],
        out_shape=[jax.ShapeDtypeStruct(shape, jnp.bfloat16) for shape in shapes],
        compiler_params=PACK_PARAMS,
        cost_estimate=SMALL,
        name="pack_queries",
    )(q)


def pack_stores_kernel(k, v, out):
    for i in range(k.shape[1] // HD):
        cols = slice(i * HD, (i + 1) * HD)
        out[:, 2 * i * HD : (2 * i + 1) * HD] = k[:, cols]
        out[:, (2 * i + 1) * HD : (2 * i + 2) * HD] = v[:, cols]


def pack_stores(k, v, n):
    rows, steps = k.shape[0], 4
    part, width = rows // steps, len(CHUNKS[n]) * HD
    return pl.pallas_call(
        pack_stores_kernel,
        grid=(steps,),
        in_specs=[pl.BlockSpec((part, width), lambda i: (i, n))] * 2,
        out_specs=pl.BlockSpec((part, 2 * width), lambda i: (i, 0)),
        out_shape=jax.ShapeDtypeStruct((rows, 2 * width), jnp.bfloat16),
        compiler_params=PACK_PARAMS,
        cost_estimate=SMALL,
        name="pack_stores",
    )(k, v)


def finish_kernel(counts, *refs):
    *parts, out_ref = refs
    head = 0
    for count, heads in counts:
        group, parts = parts[:count], parts[count:]
        for h in range(heads):
            total = group[0][h]
            if count > 1:
                total = sum(part[h].astype(jnp.float32) for part in group).astype(jnp.bfloat16)
            out_ref[:, (head + h) * QW : (head + h + 1) * QW] = total
        head += heads


def finish_call(groups):
    flat = [part for parts in groups for part in parts]
    return pl.pallas_call(
        functools.partial(finish_kernel, [(len(parts), parts[0].shape[0]) for parts in groups]),
        grid=(1,),
        in_specs=[whole(part.shape) for part in flat],
        out_specs=whole((QBLK, KVH * QW)),
        out_shape=jax.ShapeDtypeStruct((QBLK, KVH * QW), jnp.bfloat16),
        compiler_params=PARAMS,
        cost_estimate=SMALL,
        name="finish_heads",
    )(*flat)


class Order:
    def __init__(self):
        self.last = ()

    def before(self, *arrays):
        if not self.last:
            return arrays
        return lax.optimization_barrier((*arrays, *self.last))[: len(arrays)]

    def done(self, *arrays):
        self.last = arrays


def on_device(
    queries, ctx_keys, ctx_values, store_keys, store_values, block_ids, block_slot, gate_logit
):
    devices = lax.axis_size("seq")
    planes = devices // WITHIN
    me = lax.axis_index("seq")
    plane, within = me // WITHIN, me % WITHIN
    local_count = store_keys.shape[0]
    masked = devices * CAP != TOPM

    def xor(x, bits):
        return lax.ppermute(x, "seq", [(i, i ^ bits) for i in range(devices)])

    def all_planes(x):
        return [x] + [xor(x, k * WITHIN) for k in range(1, planes)]

    columns = [[p * WITHIN + w for p in range(planes)] for w in range(WITHIN)]
    keys = store_keys.reshape(local_count * MROWS, KVH * HD)
    values = store_values.reshape(local_count * MROWS, KVH * HD)
    order = Order()

    ctx_far = [xor(ctx_keys, 2), xor(ctx_values, 2)]
    ctx_near = [xor(ctx_keys, 1), xor(ctx_values, 1)]
    ids = all_planes(block_ids)
    q_first, q_second = pack_queries(queries)
    order.done(q_first)
    own = [pack_stores(*order.before(keys, values), 0)]
    order.done(own[0], *ctx_far)
    far = [xor(order.before(own[0])[0], 2)]
    own.append(pack_stores(*order.before(keys, values), 1))
    order.done(own[1])
    far.append(xor(own[1], 2))
    ctx_diag = [xor(part, 1) for part in ctx_far]
    near = [xor(part, 1) for part in own]
    diag = [None, None]

    gate = 1.0 / (1.0 + jnp.exp(-gate_logit))
    spread = [lax.all_gather(part, "seq", axis=0, axis_index_groups=columns) for part in (q_first, q_second)]

    place = jnp.stack([plane, within] + [plane] * 6).astype(jnp.int32)
    route = route_call(place, order.before(*ids), block_slot, local_count)
    order.done(route)
    place = place[None]
    info = jnp.concatenate([place, route])
    sources = [x for kind in zip((ctx_keys, ctx_values), ctx_near, ctx_far, ctx_diag, strict=True) for x in kind]

    def fetch_step(n):
        (far[n],) = order.before(far[n])
        order.done(far[n])
        diag[n] = xor(far[n], 1)

    def ctx_step(q, first, count, slots):
        args = order.before(place, q, *sources)
        uc, lse = ctx_call(args[0], args[1], args[2:], first, count, slots)
        order.done(lse)
        return uc, lse

    def mem_step(first, count, ctx_lse):
        n = place_of(first, CHUNKS)[0]
        args = order.before(info, spread[n], own[n], near[n], far[n], diag[n], own_lse, ctx_lse)
        um, lse = mem_call(*args[:2], args[2:6], *args[6:], first, count, CHUNKS[n][0] if count > 1 else first, planes, masked)
        order.done(lse)
        return um, all_planes(lse)

    def scale_step(first, um, uc, lses, scattered):
        n = place_of(first, CHUNKS)[0]
        um, uc, *lses = order.before(um, uc, *lses)
        parts = scale_call(place, um, own_uc, uc, gate, lses, first, first, scattered)
        order.done(parts[0])
        if scattered:
            return [lax.psum_scatter(parts[0], "seq", scatter_dimension=0, axis_index_groups=columns)]
        return [parts[0]] + [xor(parts[k], k * WITHIN) for k in range(1, planes)]

    own_uc, own_lse = ctx_step(queries, 0, KVH, 1)
    uc01, ctx_lse01 = ctx_step(spread[0], 0, 2, planes)
    fetch_step(0)
    um01, lses01 = mem_step(0, 2, ctx_lse01)
    coming = [scale_step(0, um01, uc01, lses01, True)]
    uc2, ctx_lse2 = ctx_step(spread[1], 2, 1, planes)
    fetch_step(1)
    uc3, ctx_lse3 = ctx_step(spread[1], 3, 1, planes)
    um2, lses2 = mem_step(2, 1, ctx_lse2)
    um3, lses3 = mem_step(3, 1, ctx_lse3)
    coming.append(scale_step(2, um2, uc2, lses2, True))
    coming.append(scale_step(3, um3, uc3, lses3, False))
    return finish_call(coming)


def solution(mesh):
    placed = (
        P(("groups", "seq"), None),
        P(("groups", "seq"), None),
        P(("groups", "seq"), None),
        P(("groups", "seq"), None, None),
        P(("groups", "seq"), None, None),
        P(("groups", "seq"), None),
        P("groups"),
        P(),
    )
    return jax.shard_map(
        on_device, mesh=mesh, in_specs=placed, out_specs=P(("groups", "seq"), None), check_vma=False
    )
```

```python
import functools

import jax
import jax.numpy as jnp
from jax import lax
from jax.experimental import pallas as pl
from jax.experimental.pallas import tpu as pltpu
from jax.sharding import PartitionSpec as P

H = 16
KVH = 4
HD = 128
QBLK = 256
MROWS = 128
TOPM = 32
CAP = 2
G = H // KVH
WITHIN = 4
LOG2E = 1.4426950408889634
SCALE = HD**-0.5 * LOG2E
MASKED = -1e30
QW = G * HD
CHUNKS = ((0, 1), (2, 3))
GROUPS = (((0, 1), "scatter"), ((2,), "direct"), ((3,), "direct"))


def scores_of(q, k):
    return lax.dot_general(q, k, (((1,), (1,)), ((), ())), preferred_element_type=jnp.float32)


def attend_heads(q, k, v, allowed, out_ref):
    keys = k.shape[0]
    vx = jnp.concatenate([v, jnp.ones((keys, HD), jnp.bfloat16)], axis=1)
    lane = lax.broadcasted_iota(jnp.int32, (QBLK, HD), 1)
    rows = jnp.zeros((QBLK, HD), jnp.float32)
    ahead = scores_of(q[:, :HD], k)
    for g in range(G):
        s = ahead
        if g + 1 < G:
            ahead = scores_of(q[:, (g + 1) * HD : (g + 2) * HD], k)
        if allowed is not None:
            s = jnp.where(allowed, s, MASKED)
        m = jnp.max(s, axis=1, keepdims=True)
        p = jnp.exp2((s - m) * SCALE).astype(jnp.bfloat16)
        o = jnp.dot(p, vx, preferred_element_type=jnp.float32)
        total = o[:, HD:]
        out_ref[0, :, g * HD : (g + 1) * HD] = (o[:, :HD] / total).astype(jnp.bfloat16)
        rows = jnp.where(lane == g, m * SCALE + jnp.log2(total), rows)
    return rows.T[:8]


def ctx_kernel(slot_base, info, q_ref, k0, k1, k2, k3, v0, v1, v2, v3, out_ref, lse_ref):
    slot = pl.program_id(1) + slot_base
    plane, within = info[0, 0], info[0, 1]
    target = jnp.bitwise_xor(plane, slot)

    def run(allowed):
        k = jnp.concatenate([k0[...], k1[...], k2[...], k3[...]], axis=0)
        v = jnp.concatenate([v0[...], v1[...], v2[...], v3[...]], axis=0)
        lse_ref[0, 0] = attend_heads(q_ref[0] if slot_base else q_ref[...], k, v, allowed, out_ref.at[0])

    if slot_base == 0:
        keys = WITHIN * QBLK
        col = lax.broadcasted_iota(jnp.int32, (QBLK, keys), 1)
        row = lax.broadcasted_iota(jnp.int32, (QBLK, keys), 0)
        key_pos = jnp.bitwise_xor(col // QBLK, within) * QBLK + col % QBLK
        run(key_pos <= within * QBLK + row)
        return

    @pl.when(target > plane)
    def _():
        run(None)

    @pl.when(target < plane)
    def _():
        out_ref[...] = jnp.zeros_like(out_ref)
        lse_ref[...] = jnp.full_like(lse_ref, MASKED)


def mem_kernel(masked, info, q_ref, s0, s1, s2, s3, own_lse_ref, ctx_lse_ref, out_ref, lse_ref, kbuf, vbuf):
    slot = pl.program_id(1)
    stores = (s0, s1, s2, s3)
    allowed = None
    keys = WITHIN * CAP * MROWS
    if masked:
        col = lax.broadcasted_iota(jnp.int32, (QBLK, keys), 1) // MROWS
        allowed = jnp.zeros((QBLK, keys), jnp.bool_)
    for n in range(WITHIN * CAP):
        entry = info[1 + slot, n]
        start = pl.multiple_of(jnp.maximum(entry, 0) * MROWS, MROWS)
        rows, to = pl.ds(start, MROWS), slice(n * MROWS, (n + 1) * MROWS)
        kbuf[to, :] = stores[n // CAP][rows, :HD]
        vbuf[to, :] = stores[n // CAP][rows, HD:]
        if masked:
            allowed = allowed | ((col == n) & (entry >= 0))
    lse_ref[0, 0] = attend_heads(q_ref[0], kbuf[...], vbuf[...], allowed, out_ref.at[0])
    lse_ref[0, 0, G:] = jnp.where(slot == 0, own_lse_ref[0, 0, :G], ctx_lse_ref[0, 0, :G])


def scale_kernel(planes, heads, first, scattered, info, um_ref, own_ref, uc_ref, gate_ref, *refs):
    lse_refs, out_refs = refs[:planes], refs[planes:]
    slot = pl.program_id(0)
    part_row = lax.broadcasted_iota(jnp.int32, (8, QBLK), 0)
    row = lax.broadcasted_iota(jnp.int32, (16, 2 * QW), 0) % 8
    spread = (row == lax.broadcasted_iota(jnp.int32, (16, 2 * QW), 1) // HD).astype(jnp.bfloat16)
    for h in range(heads):
        parts = [lse_refs[k][h, jnp.bitwise_xor(slot, k)] for k in range(planes)]
        top = functools.reduce(jnp.maximum, parts)
        total = functools.reduce(jnp.add, [jnp.exp2(p - top) for p in parts])
        weight = jnp.exp2(parts[0] - top) / total
        for g in range(G):
            gate = gate_ref[(first + h) * G + g]
            weight = jnp.where(part_row == g, weight * gate, weight)
            weight = jnp.where(part_row == G + g, weight * (1.0 - gate), weight)
        high = weight.astype(jnp.bfloat16)
        low = (weight - high.astype(jnp.float32)).astype(jnp.bfloat16)
        wide = lax.dot_general(
            jnp.concatenate([high, low], axis=0), spread, (((0,), (0,)), ((), ())), preferred_element_type=jnp.float32
        )
        for g in range(G):
            cols = slice(g * HD, (g + 1) * HD)
            term = wide[:, cols] * um_ref[h, 0, :, cols].astype(jnp.float32)
            ctx = jnp.where(slot == 0, own_ref[h, 0, :, cols], uc_ref[h, 0, :, cols])
            term += wide[:, QW + g * HD : QW + (g + 1) * HD] * ctx.astype(jnp.float32)
            term = term.astype(jnp.bfloat16)
            if scattered:
                out_refs[0][0, h, :, cols] = term
                continue
            for i, ref in enumerate(out_refs):

                @pl.when(slot == i)
                def _(ref=ref):
                    ref[h, :, cols] = term


PARAMS = pltpu.CompilerParams(vmem_limit_bytes=24 * 1024 * 1024)
PACK_PARAMS = pltpu.CompilerParams(vmem_limit_bytes=60 * 1024 * 1024)
SMALL = pl.CostEstimate(flops=1000, bytes_accessed=1000, transcendentals=0)


def place_of(head, chunks):
    return next((n, heads.index(head)) for n, heads in enumerate(chunks) if head in heads)


def whole(shape):
    return pl.BlockSpec(shape, lambda *_: (0,) * len(shape))


def query_spec(first):
    column = place_of(first, CHUNKS)[1]
    return pl.BlockSpec((1, QBLK, QW), lambda h, j, info: (jnp.bitwise_xor(info[0, 0], j), 0, column + h))


def per_head(rows, cols):
    return pl.BlockSpec((1, 1, rows, cols), lambda h, j, info: (h, j, 0, 0))


def partial_shapes(count, planes):
    return [
        jax.ShapeDtypeStruct((count, planes, QBLK, QW), jnp.bfloat16),
        jax.ShapeDtypeStruct((count, planes, 8, QBLK), jnp.float32),
    ]


def ctx_call(info, q, sources, first, count, planes):
    base = min(planes - 1, 1)
    kspec = pl.BlockSpec((QBLK, HD), lambda h, j, info: (0, first + h))
    if base:
        column = place_of(first, CHUNKS)[1]
        qspec = pl.BlockSpec((1, QBLK, QW), lambda h, j, info: (jnp.bitwise_xor(info[0, 0], j + 1), 0, column + h))
    else:
        qspec = pl.BlockSpec((QBLK, QW), lambda h, j, info: (0, first + h))
    return pl.pallas_call(
        functools.partial(ctx_kernel, base),
        grid_spec=pltpu.PrefetchScalarGridSpec(
            num_scalar_prefetch=1,
            grid=(count, planes - base),
            in_specs=[qspec] + [kspec] * (2 * WITHIN),
            out_specs=[per_head(QBLK, QW), per_head(8, QBLK)],
        ),
        out_shape=partial_shapes(count, planes - base),
        compiler_params=PACK_PARAMS,
        cost_estimate=SMALL,
        name="ctx_attend",
    )(info, q, *sources)


def mem_call(info, q, stores, own_lse, ctx_lse, first, count, chunk_first, planes, masked):
    keys = WITHIN * CAP * MROWS
    column = place_of(first, CHUNKS)[1]
    sspec = pl.BlockSpec((stores[0].shape[0], 2 * HD), lambda h, j, info: (0, column + h))
    return pl.pallas_call(
        functools.partial(mem_kernel, masked),
        grid_spec=pltpu.PrefetchScalarGridSpec(
            num_scalar_prefetch=1,
            grid=(count, planes),
            in_specs=[query_spec(first)]
            + [sspec] * WITHIN
            + [
                pl.BlockSpec((1, 1, 8, QBLK), lambda h, j, info: (first + h, 0, 0, 0)),
                pl.BlockSpec((1, 1, 8, QBLK), lambda h, j, info: (first - chunk_first + h, jnp.maximum(j - 1, 0), 0, 0)),
            ],
            out_specs=[per_head(QBLK, QW), per_head(8, QBLK)],
            scratch_shapes=[pltpu.VMEM((keys, HD), jnp.bfloat16), pltpu.VMEM((keys, HD), jnp.bfloat16)],
        ),
        out_shape=partial_shapes(count, planes),
        compiler_params=PARAMS,
        cost_estimate=SMALL,
        name="mem_attend",
    )(info, q, *stores, own_lse, ctx_lse)


def scale_call(info, um, own, uc, gate, lses, first, chunk_first, scattered):
    heads, planes = um.shape[:2]
    part = pl.BlockSpec((heads, 1, QBLK, QW), lambda j, info: (0, j, 0, 0))
    own_part = pl.BlockSpec((heads, 1, QBLK, QW), lambda j, info: (first // heads, 0, 0, 0))
    nth = (first - chunk_first) // heads
    rest = pl.BlockSpec((heads, 1, QBLK, QW), lambda j, info: (nth, jnp.maximum(j - 1, 0), 0, 0))
    if scattered:
        out_specs = [pl.BlockSpec((1, heads, QBLK, QW), lambda j, info: (jnp.bitwise_xor(info[0, 0], j), 0, 0, 0))]
        shapes = [(planes, heads, QBLK, QW)]
    else:
        shapes = [(heads, QBLK, QW)] * planes
        out_specs = [whole(shape) for shape in shapes]
    return pl.pallas_call(
        functools.partial(scale_kernel, planes, heads, first, scattered),
        grid_spec=pltpu.PrefetchScalarGridSpec(
            num_scalar_prefetch=1,
            grid=(planes,),
            in_specs=[part, own_part, rest, pl.BlockSpec(memory_space=pltpu.SMEM)] + [whole((heads, planes, 8, QBLK))] * planes,
            out_specs=out_specs,
        ),
        out_shape=[jax.ShapeDtypeStruct(shape, jnp.bfloat16) for shape in shapes],
        compiler_params=PARAMS,
        cost_estimate=SMALL,
        name="scale_mix",
    )(info, um, own, uc, gate, *lses)


def route_kernel(planes, local_count, *refs):
    ids_refs, (slot_ref, place_ref, out_ref) = refs[:planes], refs[planes:]
    entries = slot_ref.shape[0]
    plane, within = place_ref[0], place_ref[1]
    before = lax.broadcasted_iota(jnp.int32, (TOPM, TOPM), 0) <= lax.broadcasted_iota(jnp.int32, (TOPM, TOPM), 1)
    before = before.astype(jnp.float32)
    source = lax.broadcasted_iota(jnp.int32, (8, TOPM), 0)
    holder = plane * WITHIN + jnp.bitwise_xor(within, source)
    lane = lax.broadcasted_iota(jnp.int32, (1, HD), 1)
    for k in range(planes):
        hits = lax.broadcasted_iota(jnp.int32, (entries, TOPM), 0) == ids_refs[k][...]
        slots = jnp.sum(jnp.where(hits, slot_ref[...], 0), axis=0, keepdims=True)
        held = (slots // local_count == holder) & (source < WITHIN)
        rank = jnp.dot(held.astype(jnp.float32), before, preferred_element_type=jnp.float32)
        local = slots % local_count + 1
        row = jnp.zeros((1, HD), jnp.int32)
        for r in range(CAP):
            found = jnp.sum(jnp.where(held & (rank == r + 1), local, 0), axis=1, keepdims=True) - 1
            for s in range(WITHIN):
                row = jnp.where(lane == s * CAP + r, found[s : s + 1], row)
        out_ref[k : k + 1, :] = row[:, :8]


def route_call(place, ids, block_slot, local_count):
    planes = len(ids)
    return pl.pallas_call(
        functools.partial(route_kernel, planes, local_count),
        grid=(1,),
        in_specs=[whole((1, TOPM))] * planes
        + [whole((block_slot.shape[0], 1)), pl.BlockSpec(memory_space=pltpu.SMEM)],
        out_specs=whole((planes, 8)),
        out_shape=jax.ShapeDtypeStruct((planes, 8), jnp.int32),
        compiler_params=PARAMS,
        cost_estimate=SMALL,
        name="route_blocks",
    )(*ids, block_slot[:, None], place)


def pack_queries_kernel(q, out):
    out[...] = q[...]


def pack_queries(q, n):
    shape = (q.shape[0], len(CHUNKS[n]) * QW)
    return pl.pallas_call(
        pack_queries_kernel,
        grid=(1,),
        in_specs=[pl.BlockSpec(shape, lambda i: (0, n))],
        out_specs=whole(shape),
        out_shape=jax.ShapeDtypeStruct(shape, jnp.bfloat16),
        compiler_params=PACK_PARAMS,
        cost_estimate=SMALL,
        name="pack_queries",
    )(q)


def pack_stores_kernel(k, v, out):
    for i in range(k.shape[1] // HD):
        cols = slice(i * HD, (i + 1) * HD)
        out[:, 2 * i * HD : (2 * i + 1) * HD] = k[:, cols]
        out[:, (2 * i + 1) * HD : (2 * i + 2) * HD] = v[:, cols]


def pack_stores(k, v, n):
    rows, steps = k.shape[0], 4
    part, width = rows // steps, len(CHUNKS[n]) * HD
    return pl.pallas_call(
        pack_stores_kernel,
        grid=(steps,),
        in_specs=[pl.BlockSpec((part, width), lambda i: (i, n))] * 2,
        out_specs=pl.BlockSpec((part, 2 * width), lambda i: (i, 0)),
        out_shape=jax.ShapeDtypeStruct((rows, 2 * width), jnp.bfloat16),
        compiler_params=PACK_PARAMS,
        cost_estimate=SMALL,
        name="pack_stores",
    )(k, v)


def finish_kernel(counts, *refs):
    *parts, out_ref = refs
    head = 0
    for count, heads in counts:
        group, parts = parts[:count], parts[count:]
        for h in range(heads):
            total = group[0][h]
            if count > 1:
                total = sum(part[h].astype(jnp.float32) for part in group).astype(jnp.bfloat16)
            out_ref[:, (head + h) * QW : (head + h + 1) * QW] = total
        head += heads


def finish_call(groups, half, base=None):
    flat = [part for parts in groups for part in parts]
    counts = [(len(parts), parts[0].shape[0]) for parts in groups]
    given = [] if base is None else [base]

    def body(*refs):
        finish_kernel(counts, *refs[len(given) :])

    return pl.pallas_call(
        body,
        grid=(1,),
        in_specs=[pl.BlockSpec(memory_space=pl.ANY)] * len(given) + [whole(part.shape) for part in flat],
        out_specs=pl.BlockSpec((QBLK, KVH // 2 * QW), lambda i: (0, half)),
        out_shape=jax.ShapeDtypeStruct((QBLK, KVH * QW), jnp.bfloat16),
        input_output_aliases={0: 0} if given else {},
        compiler_params=PACK_PARAMS,
        cost_estimate=SMALL,
        name="finish_heads",
    )(*given, *flat)


class Order:
    def __init__(self):
        self.last = ()

    def before(self, *arrays):
        if not self.last:
            return arrays
        return lax.optimization_barrier((*arrays, *self.last))[: len(arrays)]

    def done(self, *arrays):
        self.last = arrays


def on_device(
    queries, ctx_keys, ctx_values, store_keys, store_values, block_ids, block_slot, gate_logit
):
    devices = lax.axis_size("seq")
    planes = devices // WITHIN
    me = lax.axis_index("seq")
    plane, within = me // WITHIN, me % WITHIN
    local_count = store_keys.shape[0]
    masked = devices * CAP != TOPM

    def xor(x, bits):
        return lax.ppermute(x, "seq", [(i, i ^ bits) for i in range(devices)])

    def all_planes(x):
        return [x] + [xor(x, k * WITHIN) for k in range(1, planes)]

    def between(x, plane_pairs):
        return lax.ppermute(
            x, "seq", [(a * WITHIN + w, b * WITHIN + w) for a, b in plane_pairs for w in range(WITHIN)]
        )

    columns = [[p * WITHIN + w for p in range(planes)] for w in range(WITHIN)]
    keys = store_keys.reshape(local_count * MROWS, KVH * HD)
    values = store_values.reshape(local_count * MROWS, KVH * HD)
    order = Order()

    ctx_far = [xor(ctx_keys, 2), xor(ctx_values, 2)]
    ctx_near = [xor(ctx_keys, 1), xor(ctx_values, 1)]
    ids = all_planes(block_ids)
    q_first = pack_queries(queries, 0)
    order.done(q_first)
    own = [pack_stores(*order.before(keys, values), 0)]
    order.done(own[0], *ctx_far)
    far = [xor(order.before(own[0])[0], 2)]
    own.append(pack_stores(*order.before(keys, values), 1))
    order.done(own[1])
    q_second = pack_queries(*order.before(queries), 1)
    order.done(q_second)
    far.append(xor(own[1], 2))
    ctx_diag = [xor(part, 1) for part in ctx_far]
    near = [xor(part, 1) for part in own]
    diag = [None, None]

    gate = 1.0 / (1.0 + jnp.exp(-gate_logit))
    spread = [lax.all_gather(part, "seq", axis=0, axis_index_groups=columns) for part in (q_first, q_second)]

    place = jnp.stack([plane, within] + [plane] * 6).astype(jnp.int32)
    route = route_call(place, order.before(*ids), block_slot, local_count)
    order.done(route)
    place = place[None]
    info = jnp.concatenate([place, route])
    sources = [x for kind in zip((ctx_keys, ctx_values), ctx_near, ctx_far, ctx_diag, strict=True) for x in kind]

    def fetch_step(n):
        (far[n],) = order.before(far[n])
        order.done(far[n])
        diag[n] = xor(far[n], 1)

    def ctx_step(q, first, count, slots):
        args = order.before(place, q, *sources)
        uc, lse = ctx_call(args[0], args[1], args[2:], first, count, slots)
        order.done(lse)
        return uc, lse

    def mem_step(first, count, ctx_lse):
        n = place_of(first, CHUNKS)[0]
        args = order.before(info, spread[n], own[n], near[n], far[n], diag[n], own_lse, ctx_lse)
        um, lse = mem_call(*args[:2], args[2:6], *args[6:], first, count, CHUNKS[n][0] if count > 1 else first, planes, masked)
        order.done(lse)
        return um, all_planes(lse)

    def scale_step(first, um, uc, lses, scattered):
        n = place_of(first, CHUNKS)[0]
        um, uc, *lses = order.before(um, uc, *lses)
        parts = scale_call(place, um, own_uc, uc, gate, lses, first, first, scattered)
        order.done(parts[0])
        if scattered:
            return [lax.psum_scatter(parts[0], "seq", scatter_dimension=0, axis_index_groups=columns)]
        if planes != 4:
            return [parts[0]] + [xor(parts[k], k * WITHIN) for k in range(1, planes)]
        handed = [between(parts[k], [(0, 1), (3, 2)]) for k in (3, 2)]
        summed = [
            (parts[k].astype(jnp.float32) + part.astype(jnp.float32)).astype(jnp.bfloat16)
            for k, part in zip((2, 3), handed, strict=True)
        ]
        far_parts = [between(summed[0], [(1, 3), (2, 0)]), between(summed[1], [(1, 2), (2, 1)])]
        return [parts[0], xor(parts[1], WITHIN), *far_parts]

    own_uc, own_lse = ctx_step(queries, 0, KVH, 1)
    uc01, ctx_lse01 = ctx_step(spread[0], 0, 2, planes)
    fetch_step(0)
    um01, lses01 = mem_step(0, 2, ctx_lse01)
    coming = [scale_step(0, um01, uc01, lses01, True)]
    uc2, ctx_lse2 = ctx_step(spread[1], 2, 1, planes)
    fetch_step(1)
    uc3, ctx_lse3 = ctx_step(spread[1], 3, 1, planes)
    um2, lses2 = mem_step(2, 1, ctx_lse2)
    um3, lses3 = mem_step(3, 1, ctx_lse3)
    coming.append(scale_step(2, um2, uc2, lses2, True))
    coming.append(scale_step(3, um3, uc3, lses3, False))
    return finish_call(coming[1:], 1, finish_call(coming[:1], 0))


def solution(mesh):
    placed = (
        P(("groups", "seq"), None),
        P(("groups", "seq"), None),
        P(("groups", "seq"), None),
        P(("groups", "seq"), None, None),
        P(("groups", "seq"), None, None),
        P(("groups", "seq"), None),
        P("groups"),
        P(),
    )
    return jax.shard_map(
        on_device, mesh=mesh, in_specs=placed, out_specs=P(("groups", "seq"), None), check_vma=False
    )
```

```python
import functools

import jax
import jax.numpy as jnp
from jax import lax
from jax.experimental import pallas as pl
from jax.experimental.pallas import tpu as pltpu
from jax.sharding import PartitionSpec as P

H = 16
KVH = 4
HD = 128
QBLK = 256
MROWS = 128
TOPM = 32
CAP = 2
G = H // KVH
WITHIN = 4
LOG2E = 1.4426950408889634
SCALE = HD**-0.5 * LOG2E
MASKED = -1e30
QW = G * HD
CHUNKS = ((0, 1), (2, 3))
GROUPS = (((0, 1), "scatter"), ((2,), "direct"), ((3,), "direct"))


def scores_of(q, k):
    return lax.dot_general(q, k, (((1,), (1,)), ((), ())), preferred_element_type=jnp.float32)


def attend_heads(q, k, v, allowed, out_ref):
    keys = k.shape[0]
    vx = jnp.concatenate([v, jnp.ones((keys, HD), jnp.bfloat16)], axis=1)
    lane = lax.broadcasted_iota(jnp.int32, (QBLK, HD), 1)
    rows = jnp.zeros((QBLK, HD), jnp.float32)
    ahead = scores_of(q[:, :HD], k)
    for g in range(G):
        s = ahead
        if g + 1 < G:
            ahead = scores_of(q[:, (g + 1) * HD : (g + 2) * HD], k)
        if allowed is not None:
            s = jnp.where(allowed, s, MASKED)
        m = jnp.max(s, axis=1, keepdims=True)
        p = jnp.exp2((s - m) * SCALE).astype(jnp.bfloat16)
        o = jnp.dot(p, vx, preferred_element_type=jnp.float32)
        total = o[:, HD:]
        out_ref[0, :, g * HD : (g + 1) * HD] = (o[:, :HD] / total).astype(jnp.bfloat16)
        rows = jnp.where(lane == g, m * SCALE + jnp.log2(total), rows)
    return rows.T[:8]


def ctx_kernel(slot_base, info, q_ref, k0, k1, k2, k3, v0, v1, v2, v3, out_ref, lse_ref):
    slot = pl.program_id(1) + slot_base
    plane, within = info[0, 0], info[0, 1]
    target = jnp.bitwise_xor(plane, slot)

    def run(allowed):
        k = jnp.concatenate([k0[...], k1[...], k2[...], k3[...]], axis=0)
        v = jnp.concatenate([v0[...], v1[...], v2[...], v3[...]], axis=0)
        lse_ref[0, 0] = attend_heads(q_ref[0] if slot_base else q_ref[...], k, v, allowed, out_ref.at[0])

    if slot_base == 0:
        keys = WITHIN * QBLK
        col = lax.broadcasted_iota(jnp.int32, (QBLK, keys), 1)
        row = lax.broadcasted_iota(jnp.int32, (QBLK, keys), 0)
        key_pos = jnp.bitwise_xor(col // QBLK, within) * QBLK + col % QBLK
        run(key_pos <= within * QBLK + row)
        return

    @pl.when(target > plane)
    def _():
        run(None)

    @pl.when(target < plane)
    def _():
        out_ref[...] = jnp.zeros_like(out_ref)
        lse_ref[...] = jnp.full_like(lse_ref, MASKED)


def mem_kernel(masked, info, q_ref, s0, s1, s2, s3, own_lse_ref, ctx_lse_ref, out_ref, lse_ref, kbuf, vbuf):
    slot = pl.program_id(1)
    stores = (s0, s1, s2, s3)
    allowed = None
    keys = WITHIN * CAP * MROWS
    if masked:
        col = lax.broadcasted_iota(jnp.int32, (QBLK, keys), 1) // MROWS
        allowed = jnp.zeros((QBLK, keys), jnp.bool_)
    for n in range(WITHIN * CAP):
        entry = info[1 + slot, n]
        start = pl.multiple_of(jnp.maximum(entry, 0) * MROWS, MROWS)
        rows, to = pl.ds(start, MROWS), slice(n * MROWS, (n + 1) * MROWS)
        kbuf[to, :] = stores[n // CAP][rows, :HD]
        vbuf[to, :] = stores[n // CAP][rows, HD:]
        if masked:
            allowed = allowed | ((col == n) & (entry >= 0))
    lse_ref[0, 0] = attend_heads(q_ref[0], kbuf[...], vbuf[...], allowed, out_ref.at[0])
    lse_ref[0, 0, G:] = jnp.where(slot == 0, own_lse_ref[0, 0, :G], ctx_lse_ref[0, 0, :G])


def scale_kernel(planes, heads, first, scattered, info, um_ref, own_ref, uc_ref, gate_ref, *refs):
    lse_refs, out_refs = refs[:planes], refs[planes:]
    slot = pl.program_id(0)
    part_row = lax.broadcasted_iota(jnp.int32, (8, QBLK), 0)
    row = lax.broadcasted_iota(jnp.int32, (16, 2 * QW), 0) % 8
    spread = (row == lax.broadcasted_iota(jnp.int32, (16, 2 * QW), 1) // HD).astype(jnp.bfloat16)
    for h in range(heads):
        parts = [lse_refs[k][h, jnp.bitwise_xor(slot, k)] for k in range(planes)]
        top = functools.reduce(jnp.maximum, parts)
        total = functools.reduce(jnp.add, [jnp.exp2(p - top) for p in parts])
        weight = jnp.exp2(parts[0] - top) / total
        for g in range(G):
            gate = gate_ref[(first + h) * G + g]
            weight = jnp.where(part_row == g, weight * gate, weight)
            weight = jnp.where(part_row == G + g, weight * (1.0 - gate), weight)
        high = weight.astype(jnp.bfloat16)
        low = (weight - high.astype(jnp.float32)).astype(jnp.bfloat16)
        wide = lax.dot_general(
            jnp.concatenate([high, low], axis=0), spread, (((0,), (0,)), ((), ())), preferred_element_type=jnp.float32
        )
        for g in range(G):
            cols = slice(g * HD, (g + 1) * HD)
            term = wide[:, cols] * um_ref[h, 0, :, cols].astype(jnp.float32)
            ctx = jnp.where(slot == 0, own_ref[h, 0, :, cols], uc_ref[h, 0, :, cols])
            term += wide[:, QW + g * HD : QW + (g + 1) * HD] * ctx.astype(jnp.float32)
            term = term.astype(jnp.bfloat16)
            if scattered:
                out_refs[0][0, h, :, cols] = term
                continue
            for i, ref in enumerate(out_refs):

                @pl.when(slot == i)
                def _(ref=ref):
                    ref[h, :, cols] = term


PARAMS = pltpu.CompilerParams(vmem_limit_bytes=24 * 1024 * 1024)
PACK_PARAMS = pltpu.CompilerParams(vmem_limit_bytes=60 * 1024 * 1024)
SMALL = pl.CostEstimate(flops=1000, bytes_accessed=1000, transcendentals=0)


def place_of(head, chunks):
    return next((n, heads.index(head)) for n, heads in enumerate(chunks) if head in heads)


def whole(shape):
    return pl.BlockSpec(shape, lambda *_: (0,) * len(shape))


def query_spec(first):
    column = place_of(first, CHUNKS)[1]
    return pl.BlockSpec((1, QBLK, QW), lambda h, j, info: (jnp.bitwise_xor(info[0, 0], j), 0, column + h))


def per_head(rows, cols):
    return pl.BlockSpec((1, 1, rows, cols), lambda h, j, info: (h, j, 0, 0))


def partial_shapes(count, planes):
    return [
        jax.ShapeDtypeStruct((count, planes, QBLK, QW), jnp.bfloat16),
        jax.ShapeDtypeStruct((count, planes, 8, QBLK), jnp.float32),
    ]


def ctx_call(info, q, sources, first, count, planes):
    base = min(planes - 1, 1)
    kspec = pl.BlockSpec((QBLK, HD), lambda h, j, info: (0, first + h))
    if base:
        column = place_of(first, CHUNKS)[1]
        qspec = pl.BlockSpec((1, QBLK, QW), lambda h, j, info: (jnp.bitwise_xor(info[0, 0], j + 1), 0, column + h))
    else:
        qspec = pl.BlockSpec((QBLK, QW), lambda h, j, info: (0, first + h))
    return pl.pallas_call(
        functools.partial(ctx_kernel, base),
        grid_spec=pltpu.PrefetchScalarGridSpec(
            num_scalar_prefetch=1,
            grid=(count, planes - base),
            in_specs=[qspec] + [kspec] * (2 * WITHIN),
            out_specs=[per_head(QBLK, QW), per_head(8, QBLK)],
        ),
        out_shape=partial_shapes(count, planes - base),
        compiler_params=PACK_PARAMS,
        cost_estimate=SMALL,
        name="ctx_attend",
    )(info, q, *sources)


def mem_call(info, q, stores, own_lse, ctx_lse, first, count, chunk_first, planes, masked):
    keys = WITHIN * CAP * MROWS
    column = place_of(first, CHUNKS)[1]
    sspec = pl.BlockSpec((stores[0].shape[0], 2 * HD), lambda h, j, info: (0, column + h))
    return pl.pallas_call(
        functools.partial(mem_kernel, masked),
        grid_spec=pltpu.PrefetchScalarGridSpec(
            num_scalar_prefetch=1,
            grid=(count, planes),
            in_specs=[query_spec(first)]
            + [sspec] * WITHIN
            + [
                pl.BlockSpec((1, 1, 8, QBLK), lambda h, j, info: (first + h, 0, 0, 0)),
                pl.BlockSpec((1, 1, 8, QBLK), lambda h, j, info: (first - chunk_first + h, jnp.maximum(j - 1, 0), 0, 0)),
            ],
            out_specs=[per_head(QBLK, QW), per_head(8, QBLK)],
            scratch_shapes=[pltpu.VMEM((keys, HD), jnp.bfloat16), pltpu.VMEM((keys, HD), jnp.bfloat16)],
        ),
        out_shape=partial_shapes(count, planes),
        compiler_params=PARAMS,
        cost_estimate=SMALL,
        name="mem_attend",
    )(info, q, *stores, own_lse, ctx_lse)


def scale_call(info, um, own, uc, gate, lses, first, chunk_first, scattered):
    heads, planes = um.shape[:2]
    part = pl.BlockSpec((heads, 1, QBLK, QW), lambda j, info: (0, j, 0, 0))
    own_part = pl.BlockSpec((heads, 1, QBLK, QW), lambda j, info: (first // heads, 0, 0, 0))
    nth = (first - chunk_first) // heads
    rest = pl.BlockSpec((heads, 1, QBLK, QW), lambda j, info: (nth, jnp.maximum(j - 1, 0), 0, 0))
    if scattered:
        out_specs = [pl.BlockSpec((1, heads, QBLK, QW), lambda j, info: (jnp.bitwise_xor(info[0, 0], j), 0, 0, 0))]
        shapes = [(planes, heads, QBLK, QW)]
    else:
        shapes = [(heads, QBLK, QW)] * planes
        out_specs = [whole(shape) for shape in shapes]
    return pl.pallas_call(
        functools.partial(scale_kernel, planes, heads, first, scattered),
        grid_spec=pltpu.PrefetchScalarGridSpec(
            num_scalar_prefetch=1,
            grid=(planes,),
            in_specs=[part, own_part, rest, pl.BlockSpec(memory_space=pltpu.SMEM)] + [whole((heads, planes, 8, QBLK))] * planes,
            out_specs=out_specs,
        ),
        out_shape=[jax.ShapeDtypeStruct(shape, jnp.bfloat16) for shape in shapes],
        compiler_params=PARAMS,
        cost_estimate=SMALL,
        name="scale_mix",
    )(info, um, own, uc, gate, *lses)


def route_kernel(planes, local_count, *refs):
    ids_refs, (slot_ref, place_ref, out_ref) = refs[:planes], refs[planes:]
    entries = slot_ref.shape[0]
    plane, within = place_ref[0], place_ref[1]
    before = lax.broadcasted_iota(jnp.int32, (TOPM, TOPM), 0) <= lax.broadcasted_iota(jnp.int32, (TOPM, TOPM), 1)
    before = before.astype(jnp.float32)
    source = lax.broadcasted_iota(jnp.int32, (8, TOPM), 0)
    holder = plane * WITHIN + jnp.bitwise_xor(within, source)
    lane = lax.broadcasted_iota(jnp.int32, (1, HD), 1)
    for k in range(planes):
        hits = lax.broadcasted_iota(jnp.int32, (entries, TOPM), 0) == ids_refs[k][...]
        slots = jnp.sum(jnp.where(hits, slot_ref[...], 0), axis=0, keepdims=True)
        held = (slots // local_count == holder) & (source < WITHIN)
        rank = jnp.dot(held.astype(jnp.float32), before, preferred_element_type=jnp.float32)
        local = slots % local_count + 1
        row = jnp.zeros((1, HD), jnp.int32)
        for r in range(CAP):
            found = jnp.sum(jnp.where(held & (rank == r + 1), local, 0), axis=1, keepdims=True) - 1
            for s in range(WITHIN):
                row = jnp.where(lane == s * CAP + r, found[s : s + 1], row)
        out_ref[k : k + 1, :] = row[:, :8]


def route_call(place, ids, block_slot, local_count):
    planes = len(ids)
    return pl.pallas_call(
        functools.partial(route_kernel, planes, local_count),
        grid=(1,),
        in_specs=[whole((1, TOPM))] * planes
        + [whole((block_slot.shape[0], 1)), pl.BlockSpec(memory_space=pltpu.SMEM)],
        out_specs=whole((planes, 8)),
        out_shape=jax.ShapeDtypeStruct((planes, 8), jnp.int32),
        compiler_params=PARAMS,
        cost_estimate=SMALL,
        name="route_blocks",
    )(*ids, block_slot[:, None], place)


def pack_queries_kernel(q, out):
    out[...] = q[...]


def pack_queries(q, n):
    shape = (q.shape[0], len(CHUNKS[n]) * QW)
    return pl.pallas_call(
        pack_queries_kernel,
        grid=(1,),
        in_specs=[pl.BlockSpec(shape, lambda i: (0, n))],
        out_specs=whole(shape),
        out_shape=jax.ShapeDtypeStruct(shape, jnp.bfloat16),
        compiler_params=PACK_PARAMS,
        cost_estimate=SMALL,
        name="pack_queries",
    )(q)


def pack_stores_kernel(k, v, out):
    for i in range(k.shape[1] // HD):
        cols = slice(i * HD, (i + 1) * HD)
        out[:, 2 * i * HD : (2 * i + 1) * HD] = k[:, cols]
        out[:, (2 * i + 1) * HD : (2 * i + 2) * HD] = v[:, cols]


def pack_stores(k, v, n):
    rows, steps = k.shape[0], 4
    part, width = rows // steps, len(CHUNKS[n]) * HD
    return pl.pallas_call(
        pack_stores_kernel,
        grid=(steps,),
        in_specs=[pl.BlockSpec((part, width), lambda i: (i, n))] * 2,
        out_specs=pl.BlockSpec((part, 2 * width), lambda i: (i, 0)),
        out_shape=jax.ShapeDtypeStruct((rows, 2 * width), jnp.bfloat16),
        compiler_params=PACK_PARAMS,
        cost_estimate=SMALL,
        name="pack_stores",
    )(k, v)


def finish_kernel(counts, *refs):
    *parts, out_ref = refs
    head = 0
    for count, heads in counts:
        group, parts = parts[:count], parts[count:]
        for h in range(heads):
            total = group[0][h]
            if count > 1:
                total = sum(part[h].astype(jnp.float32) for part in group).astype(jnp.bfloat16)
            out_ref[:, (head + h) * QW : (head + h + 1) * QW] = total
        head += heads


def finish_call(groups, half, base=None):
    flat = [part for parts in groups for part in parts]
    counts = [(len(parts), parts[0].shape[0]) for parts in groups]
    given = [] if base is None else [base]

    def body(*refs):
        finish_kernel(counts, *refs[len(given) :])

    return pl.pallas_call(
        body,
        grid=(1,),
        in_specs=[pl.BlockSpec(memory_space=pl.ANY)] * len(given) + [whole(part.shape) for part in flat],
        out_specs=pl.BlockSpec((QBLK, KVH // 2 * QW), lambda i: (0, half)),
        out_shape=jax.ShapeDtypeStruct((QBLK, KVH * QW), jnp.bfloat16),
        input_output_aliases={0: 0} if given else {},
        compiler_params=PACK_PARAMS,
        cost_estimate=SMALL,
        name="finish_heads",
    )(*given, *flat)


class Order:
    def __init__(self):
        self.last = ()

    def before(self, *arrays):
        if not self.last:
            return arrays
        return lax.optimization_barrier((*arrays, *self.last))[: len(arrays)]

    def done(self, *arrays):
        self.last = arrays


def on_device(
    queries, ctx_keys, ctx_values, store_keys, store_values, block_ids, block_slot, gate_logit
):
    devices = lax.axis_size("seq")
    planes = devices // WITHIN
    me = lax.axis_index("seq")
    plane, within = me // WITHIN, me % WITHIN
    local_count = store_keys.shape[0]
    masked = devices * CAP != TOPM

    def xor(x, bits):
        return lax.ppermute(x, "seq", [(i, i ^ bits) for i in range(devices)])

    def all_planes(x):
        return [x] + [xor(x, k * WITHIN) for k in range(1, planes)]

    def between(x, plane_pairs):
        return lax.ppermute(
            x, "seq", [(a * WITHIN + w, b * WITHIN + w) for a, b in plane_pairs for w in range(WITHIN)]
        )

    columns = [[p * WITHIN + w for p in range(planes)] for w in range(WITHIN)]
    keys = store_keys.reshape(local_count * MROWS, KVH * HD)
    values = store_values.reshape(local_count * MROWS, KVH * HD)
    order = Order()

    ctx_far = [xor(ctx_keys, 2), xor(ctx_values, 2)]
    ctx_near = [xor(ctx_keys, 1), xor(ctx_values, 1)]
    ids = all_planes(block_ids)
    q_first = pack_queries(queries, 0)
    order.done(q_first)
    own = [pack_stores(*order.before(keys, values), 0)]
    order.done(own[0], *ctx_far)
    far = [xor(order.before(own[0])[0], 2)]
    own.append(pack_stores(*order.before(keys, values), 1))
    order.done(own[1])
    q_second = pack_queries(*order.before(queries), 1)
    order.done(q_second)
    far.append(xor(own[1], 2))
    ctx_diag = [xor(part, 1) for part in ctx_far]
    near = [xor(part, 1) for part in own]
    diag = [None, None]

    gate = 1.0 / (1.0 + jnp.exp(-gate_logit))
    spread = [lax.all_gather(part, "seq", axis=0, axis_index_groups=columns) for part in (q_first, q_second)]

    place = jnp.stack([plane, within] + [plane] * 6).astype(jnp.int32)
    route = route_call(place, order.before(*ids), block_slot, local_count)
    order.done(route)
    place = place[None]
    info = jnp.concatenate([place, route])
    sources = [x for kind in zip((ctx_keys, ctx_values), ctx_near, ctx_far, ctx_diag, strict=True) for x in kind]

    def fetch_step(n):
        (far[n],) = order.before(far[n])
        order.done(far[n])
        diag[n] = xor(far[n], 1)

    def ctx_step(q, first, count, slots):
        args = order.before(place, q, *sources)
        uc, lse = ctx_call(args[0], args[1], args[2:], first, count, slots)
        order.done(lse)
        return uc, lse

    def mem_step(first, count, ctx_lse):
        n = place_of(first, CHUNKS)[0]
        args = order.before(info, spread[n], own[n], near[n], far[n], diag[n], own_lse, ctx_lse)
        um, lse = mem_call(*args[:2], args[2:6], *args[6:], first, count, CHUNKS[n][0] if count > 1 else first, planes, masked)
        order.done(lse)
        return um, all_planes(lse)

    def scale_step(first, um, uc, lses, scattered):
        n = place_of(first, CHUNKS)[0]
        um, uc, *lses = order.before(um, uc, *lses)
        parts = scale_call(place, um, own_uc, uc, gate, lses, first, first, scattered)
        order.done(parts[0])
        if scattered:
            return [lax.psum_scatter(parts[0], "seq", scatter_dimension=0, axis_index_groups=columns)]
        if planes != 4:
            return [parts[0]] + [xor(parts[k], k * WITHIN) for k in range(1, planes)]
        handed = [between(parts[k], [(0, 1), (3, 2)]) for k in (3, 2)]
        summed = [
            (parts[k].astype(jnp.float32) + part.astype(jnp.float32)).astype(jnp.bfloat16)
            for k, part in zip((2, 3), handed, strict=True)
        ]
        far_parts = [between(summed[0], [(1, 3), (2, 0)]), between(summed[1], [(1, 2), (2, 1)])]
        return [parts[0], xor(parts[1], WITHIN), *far_parts]

    own_uc, own_lse = ctx_step(queries, 0, KVH, 1)
    uc01, ctx_lse01 = ctx_step(spread[0], 0, 2, planes)
    fetch_step(0)
    um01, lses01 = mem_step(0, 2, ctx_lse01)
    coming = [scale_step(0, um01, uc01, lses01, True)]
    uc2, ctx_lse2 = ctx_step(spread[1], 2, 1, planes)
    fetch_step(1)
    uc3, ctx_lse3 = ctx_step(spread[1], 3, 1, planes)
    um2, lses2 = mem_step(2, 1, ctx_lse2)
    um3, lses3 = mem_step(3, 1, ctx_lse3)
    last = scale_step(3, um3, uc3, lses3, False)
    coming += [scale_step(2, um2, uc2, lses2, True), last]
    return finish_call(coming[1:], 1, finish_call(coming[:1], 0))


def solution(mesh):
    placed = (
        P(("groups", "seq"), None),
        P(("groups", "seq"), None),
        P(("groups", "seq"), None),
        P(("groups", "seq"), None, None),
        P(("groups", "seq"), None, None),
        P(("groups", "seq"), None),
        P("groups"),
        P(),
    )
    return jax.shard_map(
        on_device, mesh=mesh, in_specs=placed, out_specs=P(("groups", "seq"), None), check_vma=False
    )
```
